256 devices in a mesh: grp: 8 (over y, core), cache: 32 (over x, z).
Axes of the slice: x: 4, y: 4, z: 8, core: 2. Of those that a mesh axis runs over, the one named last changes fastest.
Arguments:
- queries: bfloat16 [2048, 4, 8192], P(('grp', 'cache')), may hold values from -6 to 6
- new_kv: bfloat16 [2048, 4, 2048], P(('grp', 'cache')), may hold values from -6 to 6
- kv_cache: bfloat16 [4096, 128, 2048], P(('grp', 'cache')), may hold values from -6 to 6
- page_owner: int32 [2048, 4], P(('grp', 'cache')), may hold values from 0 to 31, all different within a row; in each aligned block of 8 rows (0 to 7, 8 to 15, ...) at most 2 rows name the same one
- page_index: int32 [2048, 4, 1], P(('grp', 'cache')), may hold values from 0 to 15
- lengths: int32 [2048], P(('grp', 'cache')), may hold values from 1 to 512, as said below
Outputs:
- attention_out: bfloat16 [2048, 4, 8192], P(('grp', 'cache'))
The draws below stay inside these ranges and needn't reach their ends.
Inputs may be any that keep to these rules, and one draw needn't show every extreme that they name: `page_owner`: each row names 4 different owners; among the 8 rows held by one device no owner is named by more than 2 rows, and in every draw some owner is named by exactly 2 rows of some device. `lengths`: some request has exactly 512 valid tokens in every draw.
All inputs are finite; a program needn't handle non-finite values.
Results may differ from the reference program's by a relative error of at most 0.0051.
Values may be sent and summed in bfloat16 or wider, within the bound.
A program may use at most 192 MiB of HBM per device.

```python
import math
import jax
import jax.numpy as jnp
import numpy as np
from jax import lax

H = 64
KVH = 8
HD = 128
GQ = 8
STEPS = 4
PAGE = 128
SEL = 4
PPO = 1
RG = 1
P_DEV = 16
R_DEV = 8
REQS = 2048
CACHE_PAGES = 4096
CAP = 2
MAXLEN = 512
N_GRP = 8
N_CACHE = 32


def draw_queries(key, part):
    key = jax.random.fold_in(key, 11)
    entries = 2.0 * jax.random.truncated_normal(key, -3.0, 3.0, (REQS, STEPS, H, HD), jnp.float32)
    return entries.reshape(REQS, STEPS, H * HD).astype(jnp.bfloat16)


def draw_new_kv(key, part):
    key = jax.random.fold_in(key, 23)
    entries = jax.random.truncated_normal(key, -6.0, 6.0, (REQS, STEPS, 2, KVH, HD), jnp.float32)
    return entries.reshape(REQS, STEPS, 2 * KVH * HD).astype(jnp.bfloat16)


def draw_kv_cache(key, part):
    key = jax.random.fold_in(key, 41)
    entries = jax.random.truncated_normal(key, -6.0, 6.0, (CACHE_PAGES, PAGE, 2, KVH, HD), jnp.float32)
    return entries.reshape(CACHE_PAGES, PAGE, 2 * KVH * HD).astype(jnp.bfloat16)


def draw_lengths(key, part):
    key = jax.random.fold_in(key, 37)
    drawn = jax.random.randint(key, (REQS,), 1, MAXLEN + 1, dtype=jnp.int32)
    return drawn.at[0].set(MAXLEN)


def place_ends(values, rng, smallest, high):
    extent = values.shape
    place = [jax.random.randint(jax.random.fold_in(rng, axis), (), 0, extent[axis]) for axis in range(len(extent))]
    values = values.at[tuple(place)].set(smallest)
    longest = extent.index(max(extent))
    place[longest] = (place[longest] + 1) % extent[longest]
    return values.at[tuple(place)].set(high)


def deal_out(own_key, own, number, rows, count, top, most, slope):
    order = jax.random.permutation(own_key, count)
    crowded, common = load_shares(count, rows * top, most, slope, True), load_shares(count, rows * top, most, slope, False)
    places = jnp.arange(count)

    def named(tallies, rotation):
        used = int((tallies > 0).sum())
        fixed = max(1, used // 4)
        moved = fixed + (places - fixed + rotation * (used - fixed)) % max(1, count - fixed)
        return jnp.zeros((count,), jnp.int32).at[order[jnp.where(places < fixed, places, moved)]].set(jnp.asarray(tallies, jnp.int32))

    tallies = jnp.where(number % 4 == 0, named(crowded, number // 4), named(common, number - number // 4 - 1))
    mixed = jax.random.permutation(jax.random.fold_in(own, 3), count)
    donor, taker = mixed[0:count // 2 * 2:2], mixed[1:count // 2 * 2:2]
    slack = jnp.minimum(tallies[donor] - 1, most - tallies[taker]) // 2
    slack = jnp.where((donor == order[0]) | (taker == order[0]) | (tallies[taker] == 0), 0, jnp.maximum(slack, 0))
    moved = jax.random.randint(jax.random.fold_in(own, 4), (count // 2,), 0, 1 << 20) % (slack + 1)
    tallies = tallies.at[donor].add(-moved).at[taker].add(moved)
    items = jnp.searchsorted(jnp.cumsum(tallies), jnp.arange(rows * top), side="right").astype(jnp.int32)
    grid = items.reshape(top, rows).T
    grid = grid[jax.random.permutation(jax.random.fold_in(own, 1), rows)]
    rotation = jax.random.randint(jax.random.fold_in(own, 2), (rows, 1), 0, top)
    return jnp.take_along_axis(grid, (jnp.arange(top)[None, :] + rotation) % top, axis=1)


def load_shares(number_of, total, most, lean, full):
    weights = [(1 << 20) // math.isqrt(standing ** lean) + 1 for standing in range(1, number_of + 1)]
    largest = most if full else min(most, max(-(-total // number_of), total * weights[0] // sum(weights)))
    least = 1 if total - largest >= number_of - 1 else 0
    holding, surplus = [largest] + [least] * (number_of - 1), total - largest - least * (number_of - 1)
    while surplus > 0:
        movable = [i for i in range(1, number_of) if holding[i] < largest] or [i for i in range(1, number_of) if holding[i] < most]
        mass, budget = sum([weights[i] for i in movable]), surplus
        for i in movable:
            addition = min(most - holding[i], max(1, budget * weights[i] // mass), surplus)
            holding[i] = holding[i] + addition
            surplus = surplus - addition
    return np.array(holding)


def setup_inputs(seed: int = 0) -> dict:
    streams_of = jax.random.split(jax.random.key(seed), 7)
    queries = draw_queries(jax.random.fold_in(streams_of[6], 71), 0)
    new_kv = draw_new_kv(jax.random.fold_in(streams_of[6], 71), 0)
    kv_cache = draw_kv_cache(jax.random.fold_in(streams_of[6], 71), 0)
    page_owner_keys = jax.random.split(jax.random.fold_in(streams_of[3], 1), REQS // R_DEV)
    page_owner_turns = jax.random.permutation(jax.random.fold_in(streams_of[3], 3), REQS // R_DEV)
    page_owner = jax.vmap(lambda own, number: deal_out(jax.random.fold_in(streams_of[3], 2), own, number, R_DEV, N_CACHE, SEL, CAP, 2))(page_owner_keys, page_owner_turns).reshape((REQS, SEL))
    page_index = place_ends(jax.random.randint(streams_of[4], (REQS, SEL, PPO), 0, P_DEV), jax.random.fold_in(streams_of[4], 1), 0, P_DEV - 1).astype(jnp.int32)
    lengths = draw_lengths(jax.random.fold_in(streams_of[6], 71), 0)
    return dict(queries=queries, new_kv=new_kv, kv_cache=kv_cache, page_owner=page_owner, page_index=page_index, lengths=lengths)


neg_fill = -1e+30

def item_partial(query_row, panel_rows, valid_count):
    token_count = panel_rows.shape[0]
    query_heads = query_row.reshape(STEPS, KVH, GQ, HD).astype(jnp.float32)
    key_rows = panel_rows[:, :KVH * HD].reshape(token_count, KVH, HD).astype(jnp.float32)
    value_rows = panel_rows[:, KVH * HD:].reshape(token_count, KVH, HD).astype(jnp.float32)
    scores = jnp.einsum('tkgd,ukd->tkgu', query_heads, key_rows) * (1.0 / math.sqrt(HD))
    usable = jnp.arange(token_count, dtype=jnp.int32) < valid_count
    scores = jnp.where(usable, scores, neg_fill)
    highest = lax.optimization_barrier(jnp.max(scores, axis=-1))
    weights = jnp.where(usable, jnp.exp(scores - highest[..., None]), 0.0)
    weight_sum = lax.optimization_barrier(jnp.sum(weights, axis=-1))
    rounded = lax.optimization_barrier(weights.astype(jnp.bfloat16)).astype(jnp.float32)
    mixture = jnp.einsum('tkgu,ukd->tkgd', rounded, value_rows)
    normed = (mixture / jnp.maximum(weight_sum, 1.0)[..., None]).astype(jnp.bfloat16)
    return (normed.reshape(STEPS, KVH * GQ * HD), highest.reshape(STEPS, KVH * GQ), weight_sum.reshape(STEPS, KVH * GQ))

def new_partial(query_row, new_row):
    query_heads = query_row.reshape(STEPS, KVH, GQ, HD).astype(jnp.float32)
    key_rows = new_row[:, :KVH * HD].reshape(STEPS, KVH, HD).astype(jnp.float32)
    value_rows = new_row[:, KVH * HD:].reshape(STEPS, KVH, HD).astype(jnp.float32)
    scores = jnp.einsum('tkgd,ukd->tkgu', query_heads, key_rows) * (1.0 / math.sqrt(HD))
    causal = (jnp.arange(STEPS)[:, None] >= jnp.arange(STEPS)[None, :])[:, None, None, :]
    scores = jnp.where(causal, scores, neg_fill)
    highest = lax.optimization_barrier(jnp.max(scores, axis=-1))
    weights = jnp.where(causal, jnp.exp(scores - highest[..., None]), 0.0)
    weight_sum = lax.optimization_barrier(jnp.sum(weights, axis=-1))
    rounded = lax.optimization_barrier(weights.astype(jnp.bfloat16)).astype(jnp.float32)
    mixture = jnp.einsum('tkgu,ukd->tkgd', rounded, value_rows)
    return (mixture.reshape(STEPS, KVH * GQ, HD), highest.reshape(STEPS, KVH * GQ), weight_sum.reshape(STEPS, KVH * GQ))

def merge_parts(item_out, item_top, item_sum, new_mix, new_top, new_sum):
    peak_score = jnp.maximum(new_top, lax.optimization_barrier(jnp.max(item_top, axis=0)))
    item_weight = jnp.exp(item_top - peak_score[None]) * item_sum
    new_weight = jnp.exp(new_top - peak_score)
    item_values = lax.optimization_barrier(item_out).astype(jnp.float32).reshape(SEL, STEPS, KVH * GQ, HD)
    numerator = lax.optimization_barrier(jnp.sum(item_weight[..., None] * item_values, axis=0)) + new_weight[..., None] * new_mix
    denominator = lax.optimization_barrier(jnp.sum(item_weight, axis=0)) + new_weight * new_sum
    return (numerator / denominator[..., None]).astype(jnp.bfloat16).reshape(STEPS, KVH * GQ * HD)

def reference(queries, new_kv, kv_cache, page_owner, page_index, lengths):

    def home_order(table):
        trailing = table.shape[1:]
        grid_view = table.reshape((N_GRP, N_CACHE, N_GRP, RG) + trailing)
        return jnp.swapaxes(grid_view, 0, 2).reshape((REQS,) + trailing)
    owners = home_order(page_owner)
    page_ids = home_order(page_index)
    valid_len = home_order(lengths)
    group_ids = jnp.arange(REQS, dtype=jnp.int32) // RG % N_GRP
    page_rows = ((group_ids[:, None] * N_CACHE + owners)[:, :, None] * P_DEV + page_ids).astype(jnp.int32)
    item_span = PPO * PAGE
    starts = jnp.arange(SEL, dtype=jnp.int32) * item_span
    valid_counts = jnp.clip(valid_len[:, None] - starts[None, :], 0, item_span).astype(jnp.int32)

    def one_request(query_row, new_row, row_ids, counts):
        panel_rows = kv_cache[row_ids.reshape(-1)].reshape(SEL, item_span, kv_cache.shape[2])
        item_out, item_top, item_sum = jax.vmap(item_partial, in_axes=(None, 0, 0))(query_row, panel_rows, counts)
        new_mix, new_top, new_sum = new_partial(query_row, new_row)
        return merge_parts(item_out, item_top, item_sum, new_mix, new_top, new_sum)

    def one_block(packed):
        block_queries, block_new, block_rows, block_counts = packed
        return jax.vmap(one_request)(block_queries, block_new, block_rows, block_counts)
    block_count = REQS // N_GRP
    packed = (queries.reshape(block_count, N_GRP, STEPS, -1), new_kv.reshape(block_count, N_GRP, STEPS, -1), page_rows.reshape(block_count, N_GRP, SEL, PPO), valid_counts.reshape(block_count, N_GRP, SEL))
    outputs = lax.map(one_block, packed)
    return outputs.reshape(REQS, STEPS, -1)
```

```python
import math

import jax
import jax.numpy as jnp
from jax import lax
from jax.experimental import pallas as pl
from jax.experimental.pallas import tpu as pltpu
from jax.sharding import PartitionSpec as P

KVH = 8
HD = 128
GQ = 8
STEPS = 4
PAGE = 128
SEL = 4
NX = 4
NZ = 8
NG = 8
NC = NX * NZ
REQ = 8
CAP = 2
PAGES = 16
GROUP = STEPS * GQ
ROWS = KVH * GROUP
HALF = REQ // 2
NEG = -1e30
SCALE = 1.0 / math.sqrt(HD)
BF16 = jnp.bfloat16
F32 = jnp.float32
I32 = jnp.int32

L_REQ, L_PAGE, L_TOK = 0, 2, 4


def rows_to_lanes(column, eye):
    wide = jnp.broadcast_to(column, (ROWS, 128))
    top = jnp.sum(jnp.where(eye, wide[:128], 0.0), axis=0, keepdims=True)
    low = jnp.sum(jnp.where(eye, wide[128:], 0.0), axis=0, keepdims=True)
    return top, low


def lanes_to_rows(pair, eye):
    top = jnp.sum(jnp.where(eye, jnp.broadcast_to(pair[0:1], (128, 128)), 0.0), axis=1, keepdims=True)
    low = jnp.sum(jnp.where(eye, jnp.broadcast_to(pair[1:2], (128, 128)), 0.0), axis=1, keepdims=True)
    return jnp.concatenate([top, low], axis=0)


def kernel(
    q_ref,
    new_ref,
    rowtab_ref,
    coltab_ref,
    kv_hbm,
    out_ref,
    kv_ref,
    ag0,
    ag1,
    ag2,
    ag3,
    ag4,
    ag5,
    ag6,
    ag7,
    newv,
    xsend,
    recvq,
    outb,
    retb,
    stato,
    statb,
    plan_out,
    plan_in,
    midx_v,
    plan_s,
    midx_s,
    newmix,
    newstat,
    fin,
    kv_sem,
    loc_sem,
    gq_send,
    gq_recv,
    gn_send,
    gn_recv,
    pl_send,
    pl_recv,
    r_send,
    l_send,
    ag_recv,
    x_send,
    x_recv,
    o_send,
    o_recv,
    s_send,
    s_recv,
    f_send,
    f_recv,
):
    ag = [ag0, ag1, ag2, ag3, ag4, ag5, ag6, ag7]
    g = lax.axis_index("grp")
    c = lax.axis_index("cache")
    mx, mz = c // NZ, c % NZ

    def node(x, z):
        return {"cache": (x % NX) * NZ + z % NZ}

    kv_copy = pltpu.make_async_copy(kv_hbm, kv_ref, kv_sem)
    kv_copy.start()

    barrier = pltpu.get_barrier_semaphore()

    @pl.loop(1, NG)
    def _(i):
        pl.semaphore_signal(barrier, inc=1, device_id={"grp": (g + i) % NG})

    @pl.loop(1, NC)
    def _(i):
        pl.semaphore_signal(barrier, inc=1, device_id={"cache": (c + i) % NC})

    lane = lax.broadcasted_iota(I32, (NZ * 8, 128), 1)
    row = lax.broadcasted_iota(I32, (NZ * 8, 128), 0)
    owner_id = (row % 8) * NZ + row // 8
    match = (rowtab_ref[0:1, :] == owner_id) & (lane < NC)
    first = jnp.min(jnp.where(match, lane, 999), axis=1, keepdims=True)
    last = jnp.max(jnp.where(match, lane, -1), axis=1, keepdims=True)
    is0 = lane == first
    is1 = match & (lane == last) & (last > first)
    page_row = jnp.broadcast_to(rowtab_ref[1:2, :], (NZ * 8, 128))
    tok_row = jnp.broadcast_to(rowtab_ref[2:3, :], (NZ * 8, 128))
    plan = jnp.zeros((NZ * 8, 128), I32)
    for slot, here in enumerate((is0, is1)):
        for base, value in ((L_REQ, lane // SEL), (L_PAGE, page_row), (L_TOK, tok_row)):
            picked = jnp.sum(jnp.where(here, value, 0), axis=1, keepdims=True)
            plan = jnp.where(lane == base + slot, picked, plan)
    plan_out[...] = plan.reshape(NZ, 8, 128)

    e_lane = lax.broadcasted_iota(I32, (NC, 128), 1)
    e_row = lax.broadcasted_iota(I32, (NC, 128), 0)
    owner_col = coltab_ref[...]
    earlier = (owner_col == rowtab_ref[0:1, :]) & (e_lane < e_row)
    rank = jnp.max(jnp.where(earlier, 1, 0), axis=1, keepdims=True)
    hop = (owner_col % NZ + NZ - mz) % NZ
    dxs = (owner_col // NZ + NX - mx) % NX
    midx_v[...] = (hop * NX + dxs) * CAP + rank

    pl.semaphore_wait(barrier, NG - 1 + NC - 1)

    def gq_copy(i):
        return pltpu.make_async_remote_copy(
            q_ref.at[(g + i) % NG], ag0.at[g], gq_send.at[i], gq_recv.at[i], device_id={"grp": (g + i) % NG}
        )

    def gq_arrival(i):
        src = (g + NG - i) % NG
        return pltpu.make_async_remote_copy(
            q_ref.at[src], ag0.at[src], gq_send.at[i], gq_recv.at[i], device_id={"grp": (g + i) % NG}
        )

    def gn_copy(i):
        return pltpu.make_async_remote_copy(
            new_ref.at[(g + i) % NG], newv.at[g], gn_send.at[i], gn_recv.at[i], device_id={"grp": (g + i) % NG}
        )

    def gn_arrival(i):
        src = (g + NG - i) % NG
        return pltpu.make_async_remote_copy(
            new_ref.at[src], newv.at[src], gn_send.at[i], gn_recv.at[i], device_id={"grp": (g + i) % NG}
        )

    @pl.loop(1, NG)
    def _(i):
        gq_copy(i).start()

    own_q = pltpu.make_async_copy(q_ref.at[g], ag0.at[g], loc_sem.at[0])
    own_n = pltpu.make_async_copy(new_ref.at[g], newv.at[g], loc_sem.at[1])
    own_q.start()
    own_n.start()

    @pl.loop(1, NG)
    def _(i):
        gn_copy(i).start()

    def plan_copy(i):
        k, dx = i // NX, i % NX
        return pltpu.make_async_remote_copy(
            plan_out.at[(mz + k) % NZ], plan_in.at[i], pl_send.at[i], pl_recv.at[i], device_id=node(mx + dx, mz + k)
        )

    @pl.loop(1, NC)
    def _(i):
        plan_copy(i).start()

    own_p = pltpu.make_async_copy(plan_out.at[mz], plan_in.at[0], loc_sem.at[2])
    own_p.start()
    midx_copy = pltpu.make_async_copy(midx_v, midx_s, loc_sem.at[3])
    midx_copy.start()

    @pl.loop(1, NG)
    def _(i):
        gq_arrival(i).wait_recv()

    own_q.wait()

    def right(k, half):
        part = pl.ds(half * HALF, HALF)
        return pltpu.make_async_remote_copy(
            ag[k].at[part], ag[k + 1].at[part], r_send.at[k, half], ag_recv.at[k + 1, half], device_id=node(mx, mz + 1)
        )

    def left(k, half):
        part = pl.ds(half * HALF, HALF)
        to = (k - 1) % NZ
        return pltpu.make_async_remote_copy(
            ag[k].at[part], ag[to].at[part], l_send.at[k, half], ag_recv.at[to, half], device_id=node(mx, mz + NZ - 1)
        )

    moves = []

    def go(copy):
        copy.start()
        moves.append(copy)

    go(right(0, 0))
    go(left(0, 1))
    go(right(0, 1))
    go(left(0, 0))

    @pl.loop(1, NC)
    def _(i):
        plan_copy(i).wait_recv()

    own_p.wait()
    plan_read = pltpu.make_async_copy(plan_in, plan_s, loc_sem.at[4])
    plan_read.start()
    plan_read.wait()

    def x_copy(k, dx):
        return pltpu.make_async_remote_copy(
            xsend.at[k, dx - 1], recvq.at[k, dx], x_send.at[k, dx], x_recv.at[k, dx], device_id=node(mx + dx, mz)
        )

    def spread(k):
        for slot in range(CAP):
            recvq[k, 0, slot] = ag[k][plan_s[k * NX, mx, L_REQ + slot]]

        @pl.loop(1, NX)
        def _(dx):
            to = (mx + dx) % NX
            for slot in range(CAP):
                xsend[k, dx - 1, slot] = ag[k][plan_s[k * NX, to, L_REQ + slot]]
            x_copy(k, dx).start()

    spread(0)

    own_n.wait()

    @pl.loop(1, NG)
    def _(i):
        gn_arrival(i).wait_recv()

    eye = lax.broadcasted_iota(I32, (128, 128), 0) == lax.broadcasted_iota(I32, (128, 128), 1)
    n_row = lax.broadcasted_iota(I32, (ROWS, STEPS * KVH), 0)
    n_col = lax.broadcasted_iota(I32, (ROWS, STEPS * KVH), 1)
    n_ok = (n_row // GROUP == n_col % KVH) & (n_col // KVH <= (n_row % GROUP) // GQ)

    @pl.loop(0, REQ)
    def _(r):
        scores = lax.dot_general(ag0[r], newv[r, 0], (((1,), (1,)), ((), ())), preferred_element_type=F32) * SCALE
        scores = jnp.where(n_ok, scores, NEG)
        top = jnp.max(scores, axis=1, keepdims=True)
        weights = jnp.where(n_ok, jnp.exp(scores - top), 0.0)
        total = jnp.sum(weights, axis=1, keepdims=True)
        newmix[r] = jnp.dot(weights.astype(BF16), newv[r, 1], preferred_element_type=F32)
        for base, column in ((0, top), (2, total)):
            upper, lower = rows_to_lanes(column, eye)
            newstat[r, base : base + 1] = upper
            newstat[r, base + 1 : base + 2] = lower

    kv_copy.wait()

    def o_copy(k, dx):
        i = k * NX + dx
        return pltpu.make_async_remote_copy(
            outb.at[i], retb.at[pl.ds(i * CAP, CAP)], o_send.at[i], o_recv.at[i],
            device_id=node(mx + NX - dx, mz + NZ - k),
        )

    def s_copy(k, dx):
        i = k * NX + dx
        return pltpu.make_async_remote_copy(
            stato.at[i], statb.at[pl.ds(i * CAP, CAP)], s_send.at[i], s_recv.at[i],
            device_id=node(mx + NX - dx, mz + NZ - k),
        )

    token = lax.broadcasted_iota(I32, (ROWS, PAGE), 1)

    def attend(k, dx):
        i = k * NX + dx
        for slot in range(CAP):
            page = plan_s[i, mx, L_PAGE + slot]
            usable = token < plan_s[i, mx, L_TOK + slot]
            query = recvq[k, dx, slot]
            scores = jnp.concatenate(
                [
                    lax.dot_general(
                        query[e * GROUP : (e + 1) * GROUP],
                        kv_ref[page, :, e * HD : (e + 1) * HD],
                        (((1,), (1,)), ((), ())),
                        preferred_element_type=F32,
                    )
                    for e in range(KVH)
                ],
                axis=0,
            )
            scores = jnp.where(usable, scores * SCALE, NEG)
            top = jnp.max(scores, axis=1, keepdims=True)
            weights = jnp.where(usable, jnp.exp(scores - top), 0.0)
            total = jnp.sum(weights, axis=1, keepdims=True)
            rounded = weights.astype(BF16)
            for e in range(KVH):
                mixed = jnp.dot(
                    rounded[e * GROUP : (e + 1) * GROUP],
                    kv_ref[page, :, (KVH + e) * HD : (KVH + e + 1) * HD],
                    preferred_element_type=F32,
                )
                outb[i, slot, e * GROUP : (e + 1) * GROUP] = mixed.astype(BF16)
            for base, column in ((0, top), (2, total)):
                upper, lower = rows_to_lanes(column, eye)
                stato[i, slot, base : base + 1] = upper
                stato[i, slot, base + 1 : base + 2] = lower

    def work(ks):
        @pl.loop(0, len(ks) * NX)
        def _(t):
            dx = t % NX
            k = ks[0] if len(ks) == 1 else jnp.where(t < NX, ks[0], ks[1])

            @pl.when(dx > 0)
            def _():
                x_copy(k, dx).wait_recv()

            attend(k, dx)

            @pl.when(k + dx > 0)
            def _():
                o_copy(k, dx).start()
                s_copy(k, dx).start()

    steps = [(0,), (1, 7), (2, 6), (3, 5), (4,)]
    for step in range(1, 5):
        for half_a, half_b in ((0, 1), (1, 0)):
            if step < 4:
                right(step - 1, half_a).wait_recv()
                if step + 1 < 4 or half_a == 0:
                    go(right(step, half_a))
                left((NZ - step + 1) % NZ, half_b).wait_recv()
                if step + 1 < 4 or half_b == 1:
                    go(left(NZ - step, half_b))
        if step == 4:
            right(3, 0).wait_recv()
            left(5, 1).wait_recv()
        for k in steps[step]:
            spread(k)
        work(steps[step - 1])
    work(steps[4])

    own_o = pltpu.make_async_copy(outb.at[0], retb.at[pl.ds(0, CAP)], loc_sem.at[5])
    own_s = pltpu.make_async_copy(stato.at[0], statb.at[pl.ds(0, CAP)], loc_sem.at[6])
    own_o.start()
    own_s.start()
    midx_copy.wait()
    own_o.wait()
    own_s.wait()

    @pl.loop(1, NC)
    def _(i):
        o_copy(i // NX, i % NX).wait_recv()
        s_copy(i // NX, i % NX).wait_recv()

    def f_copy(i):
        to = (g + i) % NG
        return pltpu.make_async_remote_copy(
            fin.at[to], out_ref.at[g], f_send.at[i], f_recv.at[i], device_id={"grp": to}
        )

    def f_arrival(i):
        src = (g + NG - i) % NG
        return pltpu.make_async_remote_copy(
            fin.at[src], out_ref.at[src], f_send.at[i], f_recv.at[i], device_id={"grp": (g + i) % NG}
        )

    own_f = pltpu.make_async_copy(fin.at[g], out_ref.at[g], loc_sem.at[7])

    @pl.loop(0, NG)
    def _(t):
        i = (t + 1) % NG
        r = (g + i) % NG
        at = [midx_s[r * SEL + s, 0] for s in range(SEL)]
        stats = [statb[a] for a in at]
        new = newstat[r]
        peak = new[0:2]
        for stat in stats:
            peak = jnp.maximum(peak, stat[0:2])
        shares = [jnp.exp(stat[0:2] - peak) for stat in stats] + [jnp.exp(new[0:2] - peak)]
        denominator = shares[SEL] * new[2:4]
        for s in range(SEL):
            denominator = denominator + shares[s] * stats[s][2:4]
        result = lanes_to_rows(shares[SEL] / denominator, eye) * newmix[r]
        for s in range(SEL):
            result = result + lanes_to_rows(shares[s] / denominator, eye) * retb[at[s]].astype(F32)
        fin[r] = result.astype(BF16)

        @pl.when(i > 0)
        def _():
            f_copy(i).start()

        @pl.when(i == 0)
        def _():
            own_f.start()

    own_f.wait()

    for copy in moves:
        copy.wait_send()

    @pl.loop(1, NG)
    def _(i):
        gq_copy(i).wait_send()
        gn_copy(i).wait_send()

    @pl.loop(1, NC)
    def _(i):
        plan_copy(i).wait_send()
        o_copy(i // NX, i % NX).wait_send()
        s_copy(i // NX, i % NX).wait_send()

    @pl.loop(0, NZ)
    def _(k):
        for dx in range(1, NX):
            x_copy(k, dx).wait_send()

    @pl.loop(1, NG)
    def _(i):
        f_arrival(i).wait_recv()
        f_copy(i).wait_send()


def per_device(queries, new_kv, kv_cache, page_owner, page_index, lengths):
    q = queries.reshape(REQ, STEPS, KVH, GQ, HD).transpose(0, 2, 1, 3, 4).reshape(REQ, ROWS, HD)
    new = new_kv.reshape(REQ, STEPS, 2, KVH, HD).transpose(0, 2, 1, 3, 4).reshape(REQ, 2, STEPS * KVH, HD)
    starts = jnp.arange(SEL, dtype=I32) * PAGE
    counts = jnp.clip(lengths[:, None] - starts[None, :], 0, PAGE)
    owners = page_owner.reshape(1, NC)
    rows = jnp.concatenate([owners, page_index.reshape(1, NC), counts.reshape(1, NC)], axis=0)
    rowtab = jnp.pad(rows, ((0, 5), (0, 128 - NC)), constant_values=-1)
    coltab = jnp.broadcast_to(page_owner.reshape(NC, 1), (NC, 128))
    dma = pltpu.SemaphoreType.DMA
    block = pltpu.VMEM((REQ, ROWS, HD), BF16)
    vmem = pl.BlockSpec(memory_space=pltpu.VMEM)
    out = pl.pallas_call(
        kernel,
        out_shape=jax.ShapeDtypeStruct((REQ, ROWS, HD), BF16),
        in_specs=[vmem, vmem, vmem, vmem, pl.BlockSpec(memory_space=pl.ANY)],
        out_specs=pl.BlockSpec(memory_space=pl.ANY),
        scratch_shapes=[
            pltpu.VMEM((PAGES, PAGE, 2 * KVH * HD), BF16),
            *[block] * NZ,
            pltpu.VMEM((REQ, 2, STEPS * KVH, HD), BF16),
            pltpu.VMEM((NZ, NX - 1, CAP, ROWS, HD), BF16),
            pltpu.VMEM((NZ, NX, CAP, ROWS, HD), BF16),
            pltpu.VMEM((NC, CAP, ROWS, HD), BF16),
            pltpu.VMEM((NC * CAP, ROWS, HD), BF16),
            pltpu.VMEM((NC, CAP, 8, 128), F32),
            pltpu.VMEM((NC * CAP, 8, 128), F32),
            pltpu.VMEM((NZ, 8, 128), I32),
            pltpu.VMEM((NC, 8, 128), I32),
            pltpu.VMEM((NC, 128), I32),
            pltpu.SMEM((NC, 8, 128), I32),
            pltpu.SMEM((NC, 128), I32),
            pltpu.VMEM((REQ, ROWS, HD), F32),
            pltpu.VMEM((REQ, 8, 128), F32),
            block,
            dma,
            dma((8,)),
            dma((NG,)),
            dma((NG,)),
            dma((NG,)),
            dma((NG,)),
            dma((NC,)),
            dma((NC,)),
            dma((NZ, 2)),
            dma((NZ, 2)),
            dma((NZ, 2)),
            dma((NZ, NX)),
            dma((NZ, NX)),
            dma((NC,)),
            dma((NC,)),
            dma((NC,)),
            dma((NC,)),
            dma((NG,)),
            dma((NG,)),
        ],
        compiler_params=pltpu.CompilerParams(
            collective_id=0, has_side_effects=True, vmem_limit_bytes=56 * 1024 * 1024
        ),
        name="paged_decode",
    )(q, new, rowtab, coltab, kv_cache)
    out = out.reshape(REQ, KVH, STEPS, GQ, HD).transpose(0, 2, 1, 3, 4)
    return out.reshape(REQ, STEPS, KVH * GQ * HD)


def solution(mesh):
    in_specs = (
        P(("grp", "cache"), None, None),
        P(("grp", "cache"), None, None),
        P(("grp", "cache"), None, None),
        P(("grp", "cache"), None),
        P(("grp", "cache"), None, None),
        P(("grp", "cache")),
    )
    out_specs = P(("grp", "cache"), None, None)
    return jax.shard_map(
        per_device, mesh=mesh, in_specs=in_specs, out_specs=out_specs, check_vma=False
    )
```

```python
import math

import jax
import jax.numpy as jnp
from jax import lax
from jax.experimental import pallas as pl
from jax.experimental.pallas import tpu as pltpu
from jax.sharding import PartitionSpec as P

KVH = 8
HD = 128
GQ = 8
STEPS = 4
PAGE = 128
SEL = 4
NX = 4
NZ = 8
NG = 8
NC = NX * NZ
REQ = 8
CAP = 2
PAGES = 16
GROUP = STEPS * GQ
ROWS = KVH * GROUP
HALF = REQ // 2
NEG = -1e30
SCALE = 1.0 / math.sqrt(HD)
BF16 = jnp.bfloat16
F32 = jnp.float32
I32 = jnp.int32

L_REQ, L_PAGE, L_TOK, L_ID = 0, 2, 4, 6


def rows_to_lanes(column, eye):
    wide = jnp.broadcast_to(column, (ROWS, 128))
    top = jnp.sum(jnp.where(eye, wide[:128], 0.0), axis=0, keepdims=True)
    low = jnp.sum(jnp.where(eye, wide[128:], 0.0), axis=0, keepdims=True)
    return top, low


def lanes_to_rows(pair, eye):
    top = jnp.sum(jnp.where(eye, jnp.broadcast_to(pair[0:1], (128, 128)), 0.0), axis=1, keepdims=True)
    low = jnp.sum(jnp.where(eye, jnp.broadcast_to(pair[1:2], (128, 128)), 0.0), axis=1, keepdims=True)
    return jnp.concatenate([top, low], axis=0)


def kernel(
    q_ref,
    new_ref,
    rowtab_ref,
    kv_hbm,
    out_ref,
    kv_ref,
    *rest,
):
    rest = list(rest)

    def take(count):
        front = rest[:count]
        del rest[:count]
        return front

    ag, xret, xstat, dense, dstat = take(NZ), take(NZ), take(NZ), take(NZ), take(NZ)
    chain, cstat = take(NZ + 1), take(NZ + 1)
    (newv, xsend, recvq, outb, stato, plan_out, plan_in, plan_s, newmix, newstat, fin, kv_sem, loc_sem) = take(13)
    (gq_send, gq_recv, gn_send, gn_recv, pl_send, pl_recv, r_send, l_send, ag_recv, x_send, x_recv) = take(11)
    (o_send, o_recv, s_send, s_recv, c_send, c_recv, cs_send, cs_recv, f_send, f_recv) = take(10)
    ag0 = ag[0]
    g = lax.axis_index("grp")
    c = lax.axis_index("cache")
    mx, mz = c // NZ, c % NZ

    def node(x, z):
        return {"cache": (x % NX) * NZ + z % NZ}

    kv_copy = pltpu.make_async_copy(kv_hbm, kv_ref, kv_sem)
    kv_copy.start()

    barrier = pltpu.get_barrier_semaphore()

    @pl.loop(1, NG)
    def _(i):
        pl.semaphore_signal(barrier, inc=1, device_id={"grp": (g + i) % NG})

    @pl.loop(1, NC)
    def _(i):
        pl.semaphore_signal(barrier, inc=1, device_id={"cache": (c + i) % NC})

    lane = lax.broadcasted_iota(I32, (NZ * 8, 128), 1)
    row = lax.broadcasted_iota(I32, (NZ * 8, 128), 0)
    owner_id = (row % 8) * NZ + row // 8
    match = (rowtab_ref[0:1, :] == owner_id) & (lane < NC)
    first = jnp.min(jnp.where(match, lane, 999), axis=1, keepdims=True)
    last = jnp.max(jnp.where(match, lane, -1), axis=1, keepdims=True)
    is0 = lane == first
    is1 = match & (lane == last) & (last > first)
    page_row = jnp.broadcast_to(rowtab_ref[1:2, :], (NZ * 8, 128))
    tok_row = jnp.broadcast_to(rowtab_ref[2:3, :], (NZ * 8, 128))
    plan = jnp.zeros((NZ * 8, 128), I32)
    for slot, here in enumerate((is0, is1)):
        for base, value in ((L_REQ, lane // SEL), (L_PAGE, page_row), (L_TOK, tok_row)):
            picked = jnp.sum(jnp.where(here, value, 0), axis=1, keepdims=True)
            plan = jnp.where(lane == base + slot, picked, plan)
        found = jnp.max(jnp.where(here, lane // SEL, -1), axis=1, keepdims=True)
        plan = jnp.where(lane == L_ID + slot, found, plan)
    plan_out[...] = plan.reshape(NZ, 8, 128)

    pl.semaphore_wait(barrier, NG - 1 + NC - 1)

    def gq_copy(i):
        return pltpu.make_async_remote_copy(
            q_ref.at[(g + i) % NG], ag0.at[g], gq_send.at[i], gq_recv.at[i], device_id={"grp": (g + i) % NG}
        )

    def gq_arrival(i):
        src = (g + NG - i) % NG
        return pltpu.make_async_remote_copy(
            q_ref.at[src], ag0.at[src], gq_send.at[i], gq_recv.at[i], device_id={"grp": (g + i) % NG}
        )

    def gn_copy(i):
        return pltpu.make_async_remote_copy(
            new_ref.at[(g + i) % NG], newv.at[g], gn_send.at[i], gn_recv.at[i], device_id={"grp": (g + i) % NG}
        )

    def gn_arrival(i):
        src = (g + NG - i) % NG
        return pltpu.make_async_remote_copy(
            new_ref.at[src], newv.at[src], gn_send.at[i], gn_recv.at[i], device_id={"grp": (g + i) % NG}
        )

    @pl.loop(1, NG)
    def _(i):
        gq_copy(i).start()

    own_q = pltpu.make_async_copy(q_ref.at[g], ag0.at[g], loc_sem.at[0])
    own_n = pltpu.make_async_copy(new_ref.at[g], newv.at[g], loc_sem.at[1])
    own_q.start()
    own_n.start()

    @pl.loop(1, NG)
    def _(i):
        gn_copy(i).start()

    def plan_copy(i):
        k, dx = i // NX, i % NX
        return pltpu.make_async_remote_copy(
            plan_out.at[(mz + k) % NZ], plan_in.at[i], pl_send.at[i], pl_recv.at[i], device_id=node(mx + dx, mz + k)
        )

    @pl.loop(1, NC)
    def _(i):
        plan_copy(i).start()

    own_p = pltpu.make_async_copy(plan_out.at[mz], plan_in.at[0], loc_sem.at[2])
    own_p.start()

    @pl.loop(1, NG)
    def _(i):
        gq_arrival(i).wait_recv()

    own_q.wait()

    def right(k, half):
        part = pl.ds(half * HALF, HALF)
        return pltpu.make_async_remote_copy(
            ag[k].at[part], ag[k + 1].at[part], r_send.at[k, half], ag_recv.at[k + 1, half], device_id=node(mx, mz + 1)
        )

    def left(k, half):
        part = pl.ds(half * HALF, HALF)
        to = (k - 1) % NZ
        return pltpu.make_async_remote_copy(
            ag[k].at[part], ag[to].at[part], l_send.at[k, half], ag_recv.at[to, half], device_id=node(mx, mz + NZ - 1)
        )

    moves = []

    def go(copy):
        copy.start()
        moves.append(copy)

    go(right(0, 0))
    go(left(0, 1))
    go(right(0, 1))
    go(left(0, 0))

    @pl.loop(1, NC)
    def _(i):
        plan_copy(i).wait_recv()

    own_p.wait()
    plan_read = pltpu.make_async_copy(plan_in, plan_s, loc_sem.at[4])
    plan_read.start()
    plan_read.wait()

    def x_copy(k, dx):
        return pltpu.make_async_remote_copy(
            xsend.at[k, dx - 1], recvq.at[k, dx], x_send.at[k, dx], x_recv.at[k, dx], device_id=node(mx + dx, mz)
        )

    def spread(k):
        for slot in range(CAP):
            recvq[k, 0, slot] = ag[k][plan_s[k * NX, mx, L_REQ + slot]]

        @pl.loop(1, NX)
        def _(dx):
            to = (mx + dx) % NX
            for slot in range(CAP):
                xsend[k, dx - 1, slot] = ag[k][plan_s[k * NX, to, L_REQ + slot]]
            x_copy(k, dx).start()

    spread(0)

    own_n.wait()

    @pl.loop(1, NG)
    def _(i):
        gn_arrival(i).wait_recv()

    eye = lax.broadcasted_iota(I32, (128, 128), 0) == lax.broadcasted_iota(I32, (128, 128), 1)
    n_row = lax.broadcasted_iota(I32, (ROWS, STEPS * KVH), 0)
    n_col = lax.broadcasted_iota(I32, (ROWS, STEPS * KVH), 1)
    n_ok = (n_row // GROUP == n_col % KVH) & (n_col // KVH <= (n_row % GROUP) // GQ)

    @pl.loop(0, REQ)
    def _(r):
        scores = lax.dot_general(ag0[r], newv[r, 0], (((1,), (1,)), ((), ())), preferred_element_type=F32) * SCALE
        scores = jnp.where(n_ok, scores, NEG)
        top = jnp.max(scores, axis=1, keepdims=True)
        weights = jnp.where(n_ok, jnp.exp(scores - top), 0.0)
        total = jnp.sum(weights, axis=1, keepdims=True)
        newmix[r] = jnp.dot(weights.astype(BF16), newv[r, 1], preferred_element_type=F32)
        for base, column in ((0, top), (2, total)):
            upper, lower = rows_to_lanes(column, eye)
            newstat[r, base : base + 1] = upper
            newstat[r, base + 1 : base + 2] = lower

    kv_copy.wait()

    def o_copy(k, dx):
        return pltpu.make_async_remote_copy(
            outb.at[k, dx], xret[k].at[dx - 1], o_send.at[k, dx], o_recv.at[k, dx], device_id=node(mx + NX - dx, mz)
        )

    def s_copy(k, dx):
        return pltpu.make_async_remote_copy(
            stato.at[k, dx], xstat[k].at[dx - 1], s_send.at[k, dx], s_recv.at[k, dx], device_id=node(mx + NX - dx, mz)
        )

    token = lax.broadcasted_iota(I32, (ROWS, PAGE), 1)

    def attend(k, dx):
        i = k * NX + dx
        for slot in range(CAP):
            page = plan_s[i, mx, L_PAGE + slot]
            usable = token < plan_s[i, mx, L_TOK + slot]
            query = recvq[k, dx, slot]
            scores = jnp.concatenate(
                [
                    lax.dot_general(
                        query[e * GROUP : (e + 1) * GROUP],
                        kv_ref[page, :, e * HD : (e + 1) * HD],
                        (((1,), (1,)), ((), ())),
                        preferred_element_type=F32,
                    )
                    for e in range(KVH)
                ],
                axis=0,
            )
            scores = jnp.where(usable, scores * SCALE, NEG)
            top = jnp.max(scores, axis=1, keepdims=True)
            weights = jnp.where(usable, jnp.exp(scores - top), 0.0)
            total = jnp.sum(weights, axis=1, keepdims=True)
            rounded = weights.astype(BF16)
            for e in range(KVH):
                mixed = jnp.dot(
                    rounded[e * GROUP : (e + 1) * GROUP],
                    kv_ref[page, :, (KVH + e) * HD : (KVH + e + 1) * HD],
                    preferred_element_type=F32,
                )
                outb[k, dx, slot, e * GROUP : (e + 1) * GROUP] = mixed.astype(BF16)
            for base, column in ((0, top), (2, total)):
                upper, lower = rows_to_lanes(column, eye)
                stato[k, dx, slot, base : base + 1] = upper
                stato[k, dx, slot, base + 1 : base + 2] = lower

    def work(k):
        @pl.loop(0, NX)
        def _(dx):
            @pl.when(dx > 0)
            def _():
                x_copy(k, dx).wait_recv()

            attend(k, dx)

    def give(k):
        @pl.loop(1, NX)
        def _(dx):
            o_copy(k, dx).start()
            s_copy(k, dx).start()

    steps = [(0,), (1, 7), (2, 6), (3, 5), (4,)]
    for step in range(1, 5):
        for half_a, half_b in ((0, 1), (1, 0)):
            if step < 4:
                right(step - 1, half_a).wait_recv()
                if step + 1 < 4 or half_a == 0:
                    go(right(step, half_a))
                left((NZ - step + 1) % NZ, half_b).wait_recv()
                if step + 1 < 4 or half_b == 1:
                    go(left(NZ - step, half_b))
        if step == 4:
            right(3, 0).wait_recv()
            left(5, 1).wait_recv()
        for k in steps[step]:
            spread(k)
        if step == 4:
            work(3)
            give(3)
            work(5)
        else:
            for k in steps[step - 1]:
                work(k)
                if k == 0:
                    give(k)
    work(4)
    give(4)
    give(5)

    def x_parts(k, r):
        parts = []
        for dx in range(NX):
            ids = [plan_s[k * NX, (mx + dx) % NX, L_ID + slot] for slot in range(CAP)]
            slot = jnp.where(ids[1] == r, 1, 0)
            here = (ids[0] == r) | (ids[1] == r)
            if dx == 0:
                values, stat = outb[k, 0, slot], stato[k, 0, slot]
            else:
                values, stat = xret[k][dx - 1, slot], xstat[k][dx - 1, slot]
            parts.append((values, jnp.where(here, stat[0:2], NEG), jnp.where(here, stat[2:4], 0.0), here))
        return parts

    def merge(parts, new):
        peak = parts[0][1]
        for part in parts[1:]:
            peak = jnp.maximum(peak, part[1])
        if new is not None:
            peak = jnp.maximum(peak, new[1])
        shares = []
        total = jnp.zeros((2, 128), F32)
        for _, top, count, here in parts:
            share = jnp.exp(top - peak)
            if here is not None:
                share = jnp.where(here, share, 0.0)
            shares.append(share)
            total = total + share * count
        sources = [part[0] for part in parts]
        if new is not None:
            share = jnp.exp(new[1] - peak)
            total = total + share * new[2]
            shares = [one / total for one in shares + [share]]
            sources.append(new[0])
        result = None
        for share, source in zip(shares, sources):
            term = lanes_to_rows(share, eye) * source.astype(F32)
            result = term if result is None else result + term
        return result, peak, total

    def brought(slot, r):
        stat = cstat[slot][r]
        return (chain[slot][r], stat[0:2], stat[2:4], None)

    def x_done(k):
        @pl.loop(1, NX)
        def _(dx):
            o_copy(k, dx).wait_recv()
            s_copy(k, dx).wait_recv()

    def c_copies(k, half):
        part = pl.ds(half * HALF, HALF)
        inward = k - 1 if k < 4 or (k == 4 and half == 0) else k + 1
        to = node(mx, mz + NZ - 1) if inward < k else node(mx, mz + 1)
        return [
            pltpu.make_async_remote_copy(
                dense[k].at[part], chain[inward].at[part], c_send.at[k, half], c_recv.at[inward, half], device_id=to
            ),
            pltpu.make_async_remote_copy(
                dstat[k].at[part], cstat[inward].at[part], cs_send.at[k, half], cs_recv.at[inward, half], device_id=to
            ),
        ]

    def link(k):
        x_done(k)
        for half in range(2):
            if k == 3 and half == 0 or k == 5 and half == 1:
                outer = 4
            elif k in (1, 2):
                outer = k + 1
            elif k in (6, 7):
                outer = k - 1
            else:
                outer = None
            if outer is not None:
                for copy in c_copies(outer, half):
                    copy.wait_recv()

            @pl.loop(half * HALF, (half + 1) * HALF)
            def _(r):
                parts = x_parts(k, r)
                if outer is not None:
                    parts.append(brought(k, r))
                result, peak, total = merge(parts, None)
                dense[k][r] = result.astype(BF16)
                dstat[k][r, 0:2] = peak
                dstat[k][r, 2:4] = total

            for copy in c_copies(k, half):
                go(copy)

    link(4)
    give(2)
    give(6)
    link(3)
    link(5)
    give(1)
    give(7)
    link(2)
    link(6)
    link(1)
    link(7)

    def f_copy(i):
        to = (g + i) % NG
        return pltpu.make_async_remote_copy(
            fin.at[to], out_ref.at[g], f_send.at[i], f_recv.at[i], device_id={"grp": to}
        )

    def f_arrival(i):
        src = (g + NG - i) % NG
        return pltpu.make_async_remote_copy(
            fin.at[src], out_ref.at[src], f_send.at[i], f_recv.at[i], device_id={"grp": (g + i) % NG}
        )

    own_f = pltpu.make_async_copy(fin.at[g], out_ref.at[g], loc_sem.at[7])

    x_done(0)
    for outer, half in ((1, 0), (1, 1), (7, 0), (7, 1)):
        for copy in c_copies(outer, half):
            copy.wait_recv()

    @pl.loop(0, NG)
    def _(t):
        i = (t + 1) % NG
        r = (g + i) % NG
        new = newstat[r]
        parts = x_parts(0, r) + [brought(0, r), brought(NZ, r)]
        result, _, _ = merge(parts, (newmix[r], new[0:2], new[2:4]))
        fin[r] = result.astype(BF16)

        @pl.when(i > 0)
        def _():
            f_copy(i).start()

        @pl.when(i == 0)
        def _():
            own_f.start()

    own_f.wait()

    for copy in moves:
        copy.wait_send()

    @pl.loop(1, NG)
    def _(i):
        gq_copy(i).wait_send()
        gn_copy(i).wait_send()

    @pl.loop(1, NC)
    def _(i):
        plan_copy(i).wait_send()

    for k in range(NZ):

        @pl.loop(1, NX)
        def _(dx):
            x_copy(k, dx).wait_send()
            o_copy(k, dx).wait_send()
            s_copy(k, dx).wait_send()

    @pl.loop(1, NG)
    def _(i):
        f_arrival(i).wait_recv()
        f_copy(i).wait_send()


def per_device(queries, new_kv, kv_cache, page_owner, page_index, lengths):
    q = queries.reshape(REQ, STEPS, KVH, GQ, HD).transpose(0, 2, 1, 3, 4).reshape(REQ, ROWS, HD)
    new = new_kv.reshape(REQ, STEPS, 2, KVH, HD).transpose(0, 2, 1, 3, 4).reshape(REQ, 2, STEPS * KVH, HD)
    starts = jnp.arange(SEL, dtype=I32) * PAGE
    counts = jnp.clip(lengths[:, None] - starts[None, :], 0, PAGE)
    owners = page_owner.reshape(1, NC)
    rows = jnp.concatenate([owners, page_index.reshape(1, NC), counts.reshape(1, NC)], axis=0)
    rowtab = jnp.pad(rows, ((0, 5), (0, 128 - NC)), constant_values=-1)
    dma = pltpu.SemaphoreType.DMA
    block = pltpu.VMEM((REQ, ROWS, HD), BF16)
    vmem = pl.BlockSpec(memory_space=pltpu.VMEM)
    out = pl.pallas_call(
        kernel,
        out_shape=jax.ShapeDtypeStruct((REQ, ROWS, HD), BF16),
        in_specs=[vmem, vmem, vmem, pl.BlockSpec(memory_space=pl.ANY)],
        out_specs=pl.BlockSpec(memory_space=pl.ANY),
        scratch_shapes=[
            pltpu.VMEM((PAGES, PAGE, 2 * KVH * HD), BF16),
            *[block] * NZ,
            *[pltpu.VMEM((NX - 1, CAP, ROWS, HD), BF16)] * NZ,
            *[pltpu.VMEM((NX - 1, CAP, 8, 128), F32)] * NZ,
            *[block] * NZ,
            *[pltpu.VMEM((REQ, 8, 128), F32)] * NZ,
            *[block] * (NZ + 1),
            *[pltpu.VMEM((REQ, 8, 128), F32)] * (NZ + 1),
            pltpu.VMEM((REQ, 2, STEPS * KVH, HD), BF16),
            pltpu.VMEM((NZ, NX - 1, CAP, ROWS, HD), BF16),
            pltpu.VMEM((NZ, NX, CAP, ROWS, HD), BF16),
            pltpu.VMEM((NZ, NX, CAP, ROWS, HD), BF16),
            pltpu.VMEM((NZ, NX, CAP, 8, 128), F32),
            pltpu.VMEM((NZ, 8, 128), I32),
            pltpu.VMEM((NC, 8, 128), I32),
            pltpu.SMEM((NC, 8, 128), I32),
            pltpu.VMEM((REQ, ROWS, HD), F32),
            pltpu.VMEM((REQ, 8, 128), F32),
            block,
            dma,
            dma((8,)),
            *[dma((NG,))] * 4,
            *[dma((NC,))] * 2,
            *[dma((NZ, 2))] * 3,
            *[dma((NZ, NX))] * 2,
            *[dma((NZ, NX))] * 4,
            dma((NZ, 2)),
            dma((NZ + 1, 2)),
            dma((NZ, 2)),
            dma((NZ + 1, 2)),
            *[dma((NG,))] * 2,
        ],
        compiler_params=pltpu.CompilerParams(
            collective_id=0, has_side_effects=True, vmem_limit_bytes=56 * 1024 * 1024
        ),
        name="paged_decode",
    )(q, new, rowtab, kv_cache)
    out = out.reshape(REQ, KVH, STEPS, GQ, HD).transpose(0, 2, 1, 3, 4)
    return out.reshape(REQ, STEPS, KVH * GQ * HD)


def solution(mesh):
    in_specs = (
        P(("grp", "cache"), None, None),
        P(("grp", "cache"), None, None),
        P(("grp", "cache"), None, None),
        P(("grp", "cache"), None),
        P(("grp", "cache"), None, None),
        P(("grp", "cache")),
    )
    out_specs = P(("grp", "cache"), None, None)
    return jax.shard_map(
        per_device, mesh=mesh, in_specs=in_specs, out_specs=out_specs, check_vma=False
    )
```

```python
import math

import jax
import jax.numpy as jnp
from jax import lax
from jax.experimental import pallas as pl
from jax.experimental.pallas import tpu as pltpu
from jax.sharding import PartitionSpec as P

KVH = 8
HD = 128
GQ = 8
STEPS = 4
PAGE = 128
SEL = 4
NX = 4
NZ = 8
NG = 8
NC = NX * NZ
REQ = 8
CAP = 2
PAGES = 16
GROUP = STEPS * GQ
ROWS = KVH * GROUP
HALF = REQ // 2
NCH = 2
CROWS = ROWS // NCH
CHEADS = KVH // NCH
CWIDTH = CHEADS * GQ * HD
NEG = -1e30
SCALE = 1.0 / math.sqrt(HD)
BF16 = jnp.bfloat16
F32 = jnp.float32
I32 = jnp.int32

L_REQ, L_PAGE, L_TOK, L_ID = 0, 2, 4, 6


def rows_to_lanes(column, eye):
    return jnp.sum(jnp.where(eye, jnp.broadcast_to(column, (CROWS, 128)), 0.0), axis=0, keepdims=True)


def lanes_to_rows(line, eye):
    return jnp.sum(jnp.where(eye, jnp.broadcast_to(line, (CROWS, 128)), 0.0), axis=1, keepdims=True)


def kernel(q_ref, new_ref, owner_ref, page_ref, length_ref, kv_hbm, out_ref, kv_ref, *rest):
    rest = list(rest)

    def take(count):
        front = rest[:count]
        del rest[:count]
        return front

    def take_each(count):
        return [take(count) for _ in range(NCH)]

    ag, xret, xstat, dense, dstat = (take_each(NZ) for _ in range(5))
    chain, cstat = (take_each(NZ + 1) for _ in range(2))
    qs, newv, xsend, recvq, outb, stato, plan_out, plan_in, plan_s, own_s, newmix, newtop, newsum, fin = take(14)
    kv_sem, loc_sem, gq_send, gq_recv, gn_send, gn_recv, pl_send, pl_recv = take(8)
    ag_send, ag_recv, x_send, x_recv, o_send, o_recv, s_send, s_recv = take(8)
    c_send, c_recv, cs_send, cs_recv, f_send, f_recv = take(6)

    g = lax.axis_index("grp")
    c = lax.axis_index("cache")
    mx, mz = c // NZ, c % NZ

    def node(x, z):
        return {"cache": (x % NX) * NZ + z % NZ}

    barrier = pltpu.get_barrier_semaphore()

    @pl.loop(1, NG)
    def _(i):
        pl.semaphore_signal(barrier, inc=1, device_id={"grp": (g + i) % NG})

    @pl.loop(1, NC)
    def _(i):
        pl.semaphore_signal(barrier, inc=1, device_id={"cache": (c + i) % NC})

    kv_copy = pltpu.make_async_copy(kv_hbm, kv_ref, kv_sem)
    kv_copy.start()

    entry = lax.broadcasted_iota(I32, (1, 128), 1)
    owner_row = jnp.full((1, 128), -1, I32)
    page_row = jnp.zeros((1, 128), I32)
    tok_row = jnp.zeros((1, 128), I32)
    for r in range(REQ):
        for s in range(SEL):
            at = entry == r * SEL + s
            owner_row = jnp.where(at, owner_ref[s, r], owner_row)
            page_row = jnp.where(at, page_ref[s, r], page_row)
            tok_row = jnp.where(at, jnp.clip(length_ref[r] - s * PAGE, 0, PAGE), tok_row)

    shape = (NZ, 128)
    lane = lax.broadcasted_iota(I32, shape, 1)
    row = lax.broadcasted_iota(I32, shape, 0)
    owners = jnp.broadcast_to(owner_row, shape)
    pages = jnp.broadcast_to(page_row, shape)
    tokens = jnp.broadcast_to(tok_row, shape)
    plan = jnp.zeros(shape, I32)
    for x in range(NX):
        match = (owners == row + x * NZ) & (lane < NC)
        first = jnp.min(jnp.where(match, lane, 999), axis=1, keepdims=True)
        last = jnp.max(jnp.where(match, lane, -1), axis=1, keepdims=True)
        is0 = lane == first
        is1 = match & (lane == last) & (last > first)
        for slot, here in enumerate((is0, is1)):
            for base, value in ((L_REQ, lane // SEL), (L_PAGE, pages), (L_TOK, tokens)):
                picked = jnp.sum(jnp.where(here, value, 0), axis=1, keepdims=True)
                plan = jnp.where(lane == x * 8 + base + slot, picked, plan)
            found = jnp.max(jnp.where(here, lane // SEL, -1), axis=1, keepdims=True)
            plan = jnp.where(lane == x * 8 + L_ID + slot, found, plan)
    for z in range(NZ):
        plan_out[z] = plan[z : z + 1]
    own_plan = pltpu.make_async_copy(plan_out.at[mz], own_s, loc_sem.at[2 * NCH + 3])
    own_plan.start()

    @pl.loop(0, REQ)
    def _(r):
        wide = q_ref[r].astype(F32)
        rows = [wide[:, h * HD : (h + 1) * HD] for h in range(KVH * GQ)]
        qs[r] = jnp.concatenate(rows, axis=0).astype(BF16)

    pl.semaphore_wait(barrier, NG - 1 + NC - 1)

    def drain(ref, sem):
        pltpu.make_async_copy(ref, ref, sem).wait()

    def gq_copy(ch, i):
        part = pl.ds(ch * CROWS, CROWS)
        src, dst = (g + i) % NG, g
        return pltpu.make_async_remote_copy(
            qs.at[src, part], ag[ch][0].at[dst], gq_send, gq_recv.at[ch],
            device_id={"grp": (g + i) % NG},
        )

    def gn_copy(i):
        src, dst = (g + i) % NG, g
        return pltpu.make_async_remote_copy(
            new_ref.at[src], newv.at[dst], gn_send, gn_recv, device_id={"grp": (g + i) % NG}
        )

    def plan_copy(i):
        k, dx = i // NX, i % NX
        return pltpu.make_async_remote_copy(
            plan_out.at[(mz + k) % NZ], plan_in.at[i], pl_send, pl_recv, device_id=node(mx + dx, mz + k)
        )

    own_q = [
        pltpu.make_async_copy(qs.at[g, pl.ds(ch * CROWS, CROWS)], ag[ch][0].at[g], loc_sem.at[ch])
        for ch in range(NCH)
    ]
    own_n = pltpu.make_async_copy(new_ref.at[g], newv.at[g], loc_sem.at[NCH])
    own_p = pltpu.make_async_copy(plan_out.at[mz], plan_in.at[0], loc_sem.at[NCH + 1])
    for ch in range(NCH):
        own_q[ch].start()

        @pl.loop(1, NG)
        def _(i):
            gq_copy(ch, i).start()

        if ch == 0:
            own_p.start()

            @pl.loop(1, NC)
            def _(i):
                plan_copy(i).start()

    own_n.start()

    @pl.loop(1, NG)
    def _(i):
        gn_copy(i).start()

    def right(ch, k, half):
        part = pl.ds(half * HALF, HALF)
        return pltpu.make_async_remote_copy(
            ag[ch][k].at[part], ag[ch][k + 1].at[part], ag_send,
            ag_recv.at[ch * NZ + k + 1, half], device_id=node(mx, mz + 1),
        )

    def left(ch, k, half):
        part = pl.ds(half * HALF, HALF)
        to = (k - 1) % NZ
        return pltpu.make_async_remote_copy(
            ag[ch][k].at[part], ag[ch][to].at[part], ag_send,
            ag_recv.at[ch * NZ + to, half], device_id=node(mx, mz + NZ - 1),
        )

    def arrive(ch):
        drain(ag[ch][0].at[pl.ds(0, NG - 1)], gq_recv.at[ch])
        own_q[ch].wait()

    def begin(ch):
        right(ch, 0, 0).start()
        left(ch, 0, 1).start()
        right(ch, 0, 1).start()
        left(ch, 0, 0).start()

    def pass_on(ch, step):
        for half_a, half_b in ((0, 1), (1, 0)):
            if step < 4:
                right(ch, step - 1, half_a).wait_recv()
                if step + 1 < 4 or half_a == 0:
                    right(ch, step, half_a).start()
                left(ch, (NZ - step + 1) % NZ, half_b).wait_recv()
                if step + 1 < 4 or half_b == 1:
                    left(ch, NZ - step, half_b).start()
        if step == 4:
            right(ch, 3, 0).wait_recv()
            left(ch, 5, 1).wait_recv()

    def x_copy(ch, k, dx):
        return pltpu.make_async_remote_copy(
            xsend.at[ch, k, dx - 1], recvq.at[ch, k, dx], x_send, x_recv.at[ch * NZ + k],
            device_id=node(mx + dx, mz),
        )

    def spread(ch, k):
        def wanted(to, slot):
            at = to * 8 + L_REQ + slot
            return own_s[0, at] if k == 0 else plan_s[k * NX, 0, at]

        @pl.loop(1, NX)
        def _(dx):
            to = (mx + dx) % NX
            for slot in range(CAP):
                xsend[ch, k, dx - 1, slot] = ag[ch][k][wanted(to, slot)]
            x_copy(ch, k, dx).start()

        for slot in range(CAP):
            recvq[ch, k, 0, slot] = ag[ch][k][wanted(mx, slot)]

    eye = lax.broadcasted_iota(I32, (CROWS, 128), 0) == lax.broadcasted_iota(I32, (CROWS, 128), 1)

    def new_tokens(ch):
        n_row = lax.broadcasted_iota(I32, (CROWS, STEPS * CHEADS), 0)
        n_col = lax.broadcasted_iota(I32, (CROWS, STEPS * CHEADS), 1)
        n_ok = (n_row // GROUP == n_col // STEPS) & (n_col % STEPS <= n_row % STEPS)

        @pl.loop(0, REQ)
        def _(r):
            wide = newv[r].astype(F32)
            pieces = [wide[:, e * HD : (e + 1) * HD] for e in range(2 * KVH)]
            keys = jnp.concatenate(pieces[ch * CHEADS : (ch + 1) * CHEADS], axis=0).astype(BF16)
            values = jnp.concatenate(pieces[KVH + ch * CHEADS : KVH + (ch + 1) * CHEADS], axis=0).astype(BF16)
            scores = lax.dot_general(
                ag[ch][0][r], keys, (((1,), (1,)), ((), ())), preferred_element_type=F32
            ) * SCALE
            scores = jnp.where(n_ok, scores, NEG)
            top = jnp.max(scores, axis=1, keepdims=True)
            weights = jnp.where(n_ok, jnp.exp(scores - top), 0.0)
            total = jnp.sum(weights, axis=1, keepdims=True)
            newmix[ch, r] = jnp.dot(weights.astype(BF16), values, preferred_element_type=F32)
            newtop[ch, pl.ds(r, 1)] = rows_to_lanes(top, eye)
            newsum[ch, pl.ds(r, 1)] = rows_to_lanes(total, eye)

    def o_copy(ch, k, dx):
        return pltpu.make_async_remote_copy(
            outb.at[ch, k, dx], xret[ch][k].at[dx - 1], o_send, o_recv.at[ch * NZ + k],
            device_id=node(mx + NX - dx, mz),
        )

    def s_copy(ch, k, dx):
        return pltpu.make_async_remote_copy(
            stato.at[ch, k, dx], xstat[ch][k].at[dx - 1], s_send, s_recv.at[ch * NZ + k],
            device_id=node(mx + NX - dx, mz),
        )

    token = lax.broadcasted_iota(I32, (CROWS, PAGE), 1)

    def attend(ch, k, dx):
        i = k * NX + dx
        for slot in range(CAP):
            page = plan_s[i, 0, mx * 8 + L_PAGE + slot]
            usable = token < plan_s[i, 0, mx * 8 + L_TOK + slot]
            query = recvq[ch, k, dx, slot]
            scores = jnp.concatenate(
                [
                    lax.dot_general(
                        query[e * GROUP : (e + 1) * GROUP],
                        kv_ref[page, :, (ch * CHEADS + e) * HD : (ch * CHEADS + e + 1) * HD],
                        (((1,), (1,)), ((), ())),
                        preferred_element_type=F32,
                    )
                    for e in range(CHEADS)
                ],
                axis=0,
            )
            scores = jnp.where(usable, scores * SCALE, NEG)
            top = jnp.max(scores, axis=1, keepdims=True)
            weights = jnp.where(usable, jnp.exp(scores - top), 0.0)
            total = jnp.sum(weights, axis=1, keepdims=True)
            rounded = weights.astype(BF16)
            for e in range(CHEADS):
                at = KVH + ch * CHEADS + e
                mixed = jnp.dot(
                    rounded[e * GROUP : (e + 1) * GROUP],
                    kv_ref[page, :, at * HD : (at + 1) * HD],
                    preferred_element_type=F32,
                )
                outb[ch, k, dx, slot, e * GROUP : (e + 1) * GROUP] = mixed.astype(BF16)
            stato[ch, k, dx, slot : slot + 1] = rows_to_lanes(top, eye)
            stato[ch, k, dx, CAP + slot : CAP + slot + 1] = rows_to_lanes(total, eye)

    def work(ch, k):
        @pl.loop(0, NX)
        def _(dx):
            @pl.when(dx == 1)
            def _():
                drain(recvq.at[ch, k, pl.ds(1, NX - 1)], x_recv.at[ch * NZ + k])

            attend(ch, k, dx)

    def give(ch, k):
        @pl.loop(1, NX)
        def _(dx):
            o_copy(ch, k, dx).start()
            s_copy(ch, k, dx).start()

    def x_parts(ch, k, r):
        parts = []
        for dx in range(NX):
            ids = [plan_s[k * NX, 0, (mx + dx) % NX * 8 + L_ID + slot] for slot in range(CAP)]
            second = ids[1] == r
            slot = jnp.where(second, 1, 0)
            here = (ids[0] == r) | second
            if dx == 0:
                values, stat = outb[ch, k, 0, slot], stato[ch, k, 0]
            else:
                values, stat = xret[ch][k][dx - 1, slot], xstat[ch][k][dx - 1]
            top = jnp.where(second, stat[1:2], stat[0:1])
            count = jnp.where(second, stat[3:4], stat[2:3])
            parts.append((values, jnp.where(here, top, NEG), jnp.where(here, count, 0.0), here))
        return parts

    def merge(parts, new):
        peak = parts[0][1]
        for part in parts[1:]:
            peak = jnp.maximum(peak, part[1])
        if new is not None:
            peak = jnp.maximum(peak, new[1])
        shares = []
        total = jnp.zeros((1, 128), F32)
        for _, top, count, here in parts:
            share = jnp.exp(top - peak)
            if here is not None:
                share = jnp.where(here, share, 0.0)
            shares.append(share)
            total = total + share * count
        sources = [part[0] for part in parts]
        if new is not None:
            share = jnp.exp(new[1] - peak)
            total = total + share * new[2]
            shares = [one / total for one in shares + [share]]
            sources.append(new[0])
        result = None
        for share, source in zip(shares, sources):
            term = lanes_to_rows(share, eye) * source.astype(F32)
            result = term if result is None else result + term
        return result, peak, total

    def brought(ch, slot, half, rr):
        stat = cstat[ch][slot]
        return (
            chain[ch][slot][half * HALF + rr],
            stat[half, pl.ds(rr, 1), :],
            stat[half, pl.ds(HALF + rr, 1), :],
            None,
        )

    def x_done(ch, k):
        drain(xret[ch][k], o_recv.at[ch * NZ + k])
        drain(xstat[ch][k], s_recv.at[ch * NZ + k])

    def c_copies(ch, k, half):
        part = pl.ds(half * HALF, HALF)
        inward = k - 1 if k < 4 or (k == 4 and half == 0) else k + 1
        to = node(mx, mz + NZ - 1) if inward < k else node(mx, mz + 1)
        got = ch * (NZ + 1) + inward
        return [
            pltpu.make_async_remote_copy(
                dense[ch][k].at[part], chain[ch][inward].at[part], c_send, c_recv.at[got, half],
                device_id=to,
            ),
            pltpu.make_async_remote_copy(
                dstat[ch][k].at[half], cstat[ch][inward].at[half], cs_send, cs_recv.at[got, half],
                device_id=to,
            ),
        ]

    def link(ch, k):
        x_done(ch, k)
        for half in range(2):
            if k == 3 and half == 0 or k == 5 and half == 1:
                outer = 4
            elif k in (1, 2):
                outer = k + 1
            elif k in (6, 7):
                outer = k - 1
            else:
                outer = None
            if outer is not None:
                for copy in c_copies(ch, outer, half):
                    copy.wait_recv()

            @pl.loop(0, HALF)
            def _(rr):
                parts = x_parts(ch, k, half * HALF + rr)
                if outer is not None:
                    parts.append(brought(ch, k, half, rr))
                result, peak, total = merge(parts, None)
                dense[ch][k][half * HALF + rr] = result.astype(BF16)
                dstat[ch][k][half, pl.ds(rr, 1), :] = peak
                dstat[ch][k][half, pl.ds(HALF + rr, 1), :] = total

            for copy in c_copies(ch, k, half):
                copy.start()

    def f_copy(ch, i):
        part = pl.ds(ch * CWIDTH, CWIDTH)
        src, dst = (g + i) % NG, g
        return pltpu.make_async_remote_copy(
            fin.at[ch, src], out_ref.at[dst, :, part], f_send, f_recv,
            device_id={"grp": (g + i) % NG},
        )

    own_f = [
        pltpu.make_async_copy(fin.at[ch, g], out_ref.at[g, :, pl.ds(ch * CWIDTH, CWIDTH)], loc_sem.at[NCH + 3 + ch])
        for ch in range(NCH)
    ]

    def finish(ch):
        x_done(ch, 0)
        for outer, half in ((1, 0), (1, 1), (7, 0), (7, 1)):
            for copy in c_copies(ch, outer, half):
                copy.wait_recv()

        @pl.loop(1, NG + 1)
        def _(i):
            r = (g + i) % NG
            half, rr = r // HALF, r % HALF
            parts = x_parts(ch, 0, r) + [brought(ch, 0, half, rr), brought(ch, NZ, half, rr)]
            new = (newmix[ch, r], newtop[ch, pl.ds(r, 1), :], newsum[ch, pl.ds(r, 1), :])
            result, _, _ = merge(parts, new)
            pieces = [result[h * STEPS : (h + 1) * STEPS] for h in range(CHEADS * GQ)]
            fin[ch, r] = jnp.concatenate(pieces, axis=1).astype(BF16)

            @pl.when(i < NG)
            def _():
                f_copy(ch, i).start()

            @pl.when(i == NG)
            def _():
                own_f[ch].start()

    steps = [(0,), (1, 7), (2, 6), (3, 5), (4,)]

    def forward(ch, step, todo):
        pass_on(ch, step)
        if step == 3 and ch + 1 < NCH:
            begin(ch + 1)
        for k in steps[step]:
            spread(ch, k)
        for one, k in todo:
            work(one, k)

    arrive(0)
    begin(0)
    own_plan.wait()
    spread(0, 0)
    arrive(1)
    spread(1, 0)
    pass_on(0, 1)

    drain(plan_in.at[pl.ds(0, NC - 1)], pl_recv)
    own_p.wait()
    plan_read = pltpu.make_async_copy(plan_in, plan_s, loc_sem.at[NCH + 2])
    plan_read.start()
    plan_read.wait()
    spread(0, 1)
    spread(0, 7)
    kv_copy.wait()
    work(0, 0)
    give(0, 0)
    forward(0, 2, [(1, 0)])
    own_n.wait()

    drain(newv.at[pl.ds(0, NG - 1)], gn_recv)
    forward(0, 3, [(0, 1), (0, 7)])
    forward(0, 4, [(0, 2), (0, 6)])
    forward(1, 1, [(0, 3), (0, 5)])
    forward(1, 2, [(0, 4)])
    give(0, 4)
    give(0, 3)
    give(0, 5)
    forward(1, 3, [(1, 1), (1, 7)])
    new_tokens(0)
    link(0, 4)
    forward(1, 4, [(1, 2), (1, 6)])
    give(0, 2)
    give(0, 6)
    link(0, 3)
    link(0, 5)
    work(1, 3)
    work(1, 5)
    give(0, 1)
    give(0, 7)
    link(0, 2)
    link(0, 6)
    work(1, 4)
    give(1, 4)
    give(1, 3)
    give(1, 5)
    link(0, 1)
    link(0, 7)
    link(1, 4)
    give(1, 2)
    give(1, 6)
    new_tokens(1)
    link(1, 3)
    link(1, 5)
    give(1, 1)
    give(1, 7)
    give(1, 0)
    finish(0)
    link(1, 2)
    link(1, 6)
    link(1, 1)
    link(1, 7)
    finish(1)

    for ch in range(NCH):
        own_f[ch].wait()
    drain(out_ref.at[pl.ds(0, NG - 1)], f_recv)
    drain(qs.at[pl.ds(0, NG - 1)], gq_send)
    drain(newv.at[pl.ds(0, NG - 1)], gn_send)
    drain(plan_in.at[pl.ds(0, NC - 1)], pl_send)
    drain(recvq.at[:, pl.ds(0, NZ - 1)], ag_send)
    drain(xsend, x_send)
    drain(xsend, o_send)
    drain(stato.at[:, :, pl.ds(1, NX - 1)], s_send)
    drain(recvq.at[:, pl.ds(0, NZ - 1)], c_send)
    drain(newmix.at[0, pl.ds(0, NZ - 1), pl.ds(0, 16 * NCH)], cs_send)
    drain(fin.at[:, pl.ds(0, NG - 1)], f_send)


def per_device(queries, new_kv, kv_cache, page_owner, page_index, lengths):
    dma = pltpu.SemaphoreType.DMA
    vmem = pl.BlockSpec(memory_space=pltpu.VMEM)
    smem = pl.BlockSpec(memory_space=pltpu.SMEM)
    hbm = pl.BlockSpec(memory_space=pl.ANY)
    block = pltpu.VMEM((REQ, CROWS, HD), BF16)
    return pl.pallas_call(
        kernel,
        out_shape=jax.ShapeDtypeStruct((REQ, STEPS, KVH * GQ * HD), BF16),
        in_specs=[vmem, vmem, smem, smem, smem, hbm],
        out_specs=hbm,
        scratch_shapes=[
            pltpu.VMEM((PAGES, PAGE, 2 * KVH * HD), BF16),
            *[block] * (NCH * NZ),
            *[pltpu.VMEM((NX - 1, CAP, CROWS, HD), BF16)] * (NCH * NZ),
            *[pltpu.VMEM((NX - 1, 2 * CAP, 128), F32)] * (NCH * NZ),
            *[block] * (NCH * NZ),
            *[pltpu.VMEM((2, 8, 128), F32)] * (NCH * NZ),
            *[block] * (NCH * (NZ + 1)),
            *[pltpu.VMEM((2, 8, 128), F32)] * (NCH * (NZ + 1)),
            pltpu.VMEM((REQ, ROWS, HD), BF16),
            pltpu.VMEM((REQ, STEPS, 2 * KVH * HD), BF16),
            pltpu.VMEM((NCH, NZ, NX - 1, CAP, CROWS, HD), BF16),
            pltpu.VMEM((NCH, NZ, NX, CAP, CROWS, HD), BF16),
            pltpu.VMEM((NCH, NZ, NX, CAP, CROWS, HD), BF16),
            pltpu.VMEM((NCH, NZ, NX, 2 * CAP, 128), F32),
            pltpu.VMEM((NZ, 1, 128), I32),
            pltpu.VMEM((NC, 1, 128), I32),
            pltpu.SMEM((NC, 1, 128), I32),
            pltpu.SMEM((1, 128), I32),
            pltpu.VMEM((NCH, REQ, CROWS, HD), F32),
            pltpu.VMEM((NCH, REQ, 128), F32),
            pltpu.VMEM((NCH, REQ, 128), F32),
            pltpu.VMEM((NCH, REQ, STEPS, CWIDTH), BF16),
            dma,
            dma((2 * NCH + 4,)),
            dma,
            dma((NCH,)),
            *[dma] * 4,
            dma,
            dma((NCH * NZ, 2)),
            *[dma, dma((NCH * NZ,))] * 3,
            *[dma, dma((NCH * (NZ + 1), 2))] * 2,
            *[dma] * 2,
        ],
        compiler_params=pltpu.CompilerParams(
            collective_id=0, has_side_effects=True, vmem_limit_bytes=56 * 1024 * 1024
        ),
        name="paged_decode",
    )(queries, new_kv, page_owner.T, page_index.reshape(REQ, SEL).T, lengths, kv_cache)


def solution(mesh):
    in_specs = (
        P(("grp", "cache"), None, None),
        P(("grp", "cache"), None, None),
        P(("grp", "cache"), None, None),
        P(("grp", "cache"), None),
        P(("grp", "cache"), None, None),
        P(("grp", "cache")),
    )
    out_specs = P(("grp", "cache"), None, None)
    return jax.shard_map(
        per_device, mesh=mesh, in_specs=in_specs, out_specs=out_specs, check_vma=False
    )
```

```python
import math

import jax
import jax.numpy as jnp
from jax import lax
from jax.experimental import pallas as pl
from jax.experimental.pallas import tpu as pltpu
from jax.sharding import PartitionSpec as P

KVH = 8
HD = 128
GQ = 8
STEPS = 4
PAGE = 128
SEL = 4
NX = 4
NZ = 8
NG = 8
NC = NX * NZ
REQ = 8
CAP = 2
PAGES = 16
GROUP = STEPS * GQ
ROWS = KVH * GROUP
HALF = REQ // 2
NCH = 2
CROWS = ROWS // NCH
CHEADS = KVH // NCH
CWIDTH = CHEADS * GQ * HD
NEG = -1e30
SCALE = 1.0 / math.sqrt(HD)
BF16 = jnp.bfloat16
F32 = jnp.float32
I32 = jnp.int32

L_REQ, L_PAGE, L_TOK, L_ID = 0, 2, 4, 6


def rows_to_lanes(column, eye):
    return jnp.sum(jnp.where(eye, jnp.broadcast_to(column, (CROWS, 128)), 0.0), axis=0, keepdims=True)


def lanes_to_rows(line, eye):
    return jnp.sum(jnp.where(eye, jnp.broadcast_to(line, (CROWS, 128)), 0.0), axis=1, keepdims=True)


def kernel(q_ref, new_ref, owner_ref, page_ref, length_ref, kv_hbm, out_ref, kv_ref, *rest):
    rest = list(rest)

    def take(count):
        front = rest[:count]
        del rest[:count]
        return front

    def take_each(count):
        return [take(count) for _ in range(NCH)]

    ag, xret, xstat, dense, dstat = (take_each(NZ) for _ in range(5))
    chain, cstat = (take_each(NZ + 1) for _ in range(2))
    qs, newv, xsend, recvq, outb, stato, plan_out, plan_in, plan_s, own_s, newmix, newtop, newsum, fin = take(14)
    kv_sem, loc_sem, gq_send, gq_recv, gn_send, gn_recv, pl_send, pl_recv = take(8)
    ag_send, ag_recv, x_send, x_recv, o_send, o_recv, s_send, s_recv = take(8)
    c_send, c_recv, cs_send, cs_recv, f_send, f_recv = take(6)

    g = lax.axis_index("grp")
    c = lax.axis_index("cache")
    mx, mz = c // NZ, c % NZ

    def node(x, z):
        return {"cache": (x % NX) * NZ + z % NZ}

    barrier = pltpu.get_barrier_semaphore()

    @pl.loop(1, NG)
    def _(i):
        pl.semaphore_signal(barrier, inc=1, device_id={"grp": (g + i) % NG})

    @pl.loop(1, NC)
    def _(i):
        pl.semaphore_signal(barrier, inc=1, device_id={"cache": (c + i) % NC})

    kv_copy = pltpu.make_async_copy(kv_hbm, kv_ref, kv_sem)
    kv_copy.start()

    def make_rows(ch):
        @pl.loop(0, REQ)
        def _(r):
            wide = q_ref[r, :, ch * CWIDTH : (ch + 1) * CWIDTH].astype(F32)
            rows = [wide[:, h * HD : (h + 1) * HD] for h in range(CHEADS * GQ)]
            qs[r, ch * CROWS : (ch + 1) * CROWS] = jnp.concatenate(rows, axis=0).astype(BF16)

    make_rows(0)
    pl.semaphore_wait(barrier, NG - 1 + NC - 1)

    def drain(ref, sem):
        pltpu.make_async_copy(ref, ref, sem).wait()

    def gq_copy(ch, i):
        part = pl.ds(ch * CROWS, CROWS)
        src, dst = (g + i) % NG, g
        return pltpu.make_async_remote_copy(
            qs.at[src, part], ag[ch][0].at[dst], gq_send, gq_recv.at[ch],
            device_id={"grp": (g + i) % NG},
        )

    def gn_copy(i):
        src, dst = (g + i) % NG, g
        return pltpu.make_async_remote_copy(
            new_ref.at[src], newv.at[dst], gn_send, gn_recv, device_id={"grp": (g + i) % NG}
        )

    def plan_copy(i):
        k, dx = i // NX, i % NX
        return pltpu.make_async_remote_copy(
            plan_out.at[(mz + k) % NZ], plan_in.at[i], pl_send, pl_recv, device_id=node(mx + dx, mz + k)
        )

    own_q = [
        pltpu.make_async_copy(qs.at[g, pl.ds(ch * CROWS, CROWS)], ag[ch][0].at[g], loc_sem.at[ch])
        for ch in range(NCH)
    ]
    own_n = pltpu.make_async_copy(new_ref.at[g], newv.at[g], loc_sem.at[NCH])
    own_p = pltpu.make_async_copy(plan_out.at[mz], plan_in.at[0], loc_sem.at[NCH + 1])
    for ch in range(NCH):
        if ch > 0:
            make_rows(ch)
        own_q[ch].start()

        @pl.loop(1, NG)
        def _(i):
            gq_copy(ch, i).start()

        if ch == 0:
            entry = lax.broadcasted_iota(I32, (1, 128), 1)
            owner_row = jnp.full((1, 128), -1, I32)
            page_row = jnp.zeros((1, 128), I32)
            tok_row = jnp.zeros((1, 128), I32)
            for r in range(REQ):
                for s in range(SEL):
                    at = entry == r * SEL + s
                    owner_row = jnp.where(at, owner_ref[s, r], owner_row)
                    page_row = jnp.where(at, page_ref[s, r], page_row)
                    tok_row = jnp.where(at, jnp.clip(length_ref[r] - s * PAGE, 0, PAGE), tok_row)

            shape = (NZ, 128)
            lane = lax.broadcasted_iota(I32, shape, 1)
            row = lax.broadcasted_iota(I32, shape, 0)
            owners = jnp.broadcast_to(owner_row, shape)
            pages = jnp.broadcast_to(page_row, shape)
            tokens = jnp.broadcast_to(tok_row, shape)
            plan = jnp.zeros(shape, I32)
            for x in range(NX):
                match = (owners == row + x * NZ) & (lane < NC)
                first = jnp.min(jnp.where(match, lane, 999), axis=1, keepdims=True)
                last = jnp.max(jnp.where(match, lane, -1), axis=1, keepdims=True)
                is0 = lane == first
                is1 = match & (lane == last) & (last > first)
                for slot, here in enumerate((is0, is1)):
                    for base, value in ((L_REQ, lane // SEL), (L_PAGE, pages), (L_TOK, tokens)):
                        picked = jnp.sum(jnp.where(here, value, 0), axis=1, keepdims=True)
                        plan = jnp.where(lane == x * 8 + base + slot, picked, plan)
                    found = jnp.max(jnp.where(here, lane // SEL, -1), axis=1, keepdims=True)
                    plan = jnp.where(lane == x * 8 + L_ID + slot, found, plan)
            for z in range(NZ):
                plan_out[z] = plan[z : z + 1]
            own_plan = pltpu.make_async_copy(plan_out.at[mz], own_s, loc_sem.at[2 * NCH + 3])
            own_plan.start()
            own_p.start()

            @pl.loop(1, NC)
            def _(i):
                plan_copy(i).start()

    own_n.start()

    @pl.loop(1, NG)
    def _(i):
        gn_copy(i).start()

    def right(ch, k, half):
        part = pl.ds(half * HALF, HALF)
        return pltpu.make_async_remote_copy(
            ag[ch][k].at[part], ag[ch][k + 1].at[part], ag_send,
            ag_recv.at[ch * NZ + k + 1, half], device_id=node(mx, mz + 1),
        )

    def left(ch, k, half):
        part = pl.ds(half * HALF, HALF)
        to = (k - 1) % NZ
        return pltpu.make_async_remote_copy(
            ag[ch][k].at[part], ag[ch][to].at[part], ag_send,
            ag_recv.at[ch * NZ + to, half], device_id=node(mx, mz + NZ - 1),
        )

    def arrive(ch):
        drain(ag[ch][0].at[pl.ds(0, NG - 1)], gq_recv.at[ch])
        own_q[ch].wait()

    def begin(ch):
        right(ch, 0, 0).start()
        left(ch, 0, 1).start()
        right(ch, 0, 1).start()
        left(ch, 0, 0).start()

    def pass_on(ch, step):
        for half_a, half_b in ((0, 1), (1, 0)):
            if step < 4:
                right(ch, step - 1, half_a).wait_recv()
                if step + 1 < 4 or half_a == 0:
                    right(ch, step, half_a).start()
                left(ch, (NZ - step + 1) % NZ, half_b).wait_recv()
                if step + 1 < 4 or half_b == 1:
                    left(ch, NZ - step, half_b).start()
        if step == 4:
            right(ch, 3, 0).wait_recv()
            left(ch, 5, 1).wait_recv()

    def x_copy(ch, k, dx):
        return pltpu.make_async_remote_copy(
            xsend.at[ch, k, dx - 1], recvq.at[ch, k, dx], x_send, x_recv.at[ch * NZ + k],
            device_id=node(mx + dx, mz),
        )

    def spread(ch, k):
        def wanted(to, slot):
            at = to * 8 + L_REQ + slot
            return own_s[0, at] if k == 0 else plan_s[k * NX, 0, at]

        @pl.loop(1, NX)
        def _(dx):
            to = (mx + dx) % NX
            for slot in range(CAP):
                xsend[ch, k, dx - 1, slot] = ag[ch][k][wanted(to, slot)]
            x_copy(ch, k, dx).start()

        for slot in range(CAP):
            recvq[ch, k, 0, slot] = ag[ch][k][wanted(mx, slot)]

    eye = lax.broadcasted_iota(I32, (CROWS, 128), 0) == lax.broadcasted_iota(I32, (CROWS, 128), 1)

    def new_tokens(ch):
        n_row = lax.broadcasted_iota(I32, (CROWS, STEPS * CHEADS), 0)
        n_col = lax.broadcasted_iota(I32, (CROWS, STEPS * CHEADS), 1)
        n_ok = (n_row // GROUP == n_col // STEPS) & (n_col % STEPS <= n_row % STEPS)

        @pl.loop(0, REQ)
        def _(r):
            wide = newv[r].astype(F32)
            pieces = [wide[:, e * HD : (e + 1) * HD] for e in range(2 * KVH)]
            keys = jnp.concatenate(pieces[ch * CHEADS : (ch + 1) * CHEADS], axis=0).astype(BF16)
            values = jnp.concatenate(pieces[KVH + ch * CHEADS : KVH + (ch + 1) * CHEADS], axis=0).astype(BF16)
            scores = lax.dot_general(
                ag[ch][0][r], keys, (((1,), (1,)), ((), ())), preferred_element_type=F32
            ) * SCALE
            scores = jnp.where(n_ok, scores, NEG)
            top = jnp.max(scores, axis=1, keepdims=True)
            weights = jnp.where(n_ok, jnp.exp(scores - top), 0.0)
            total = jnp.sum(weights, axis=1, keepdims=True)
            newmix[ch, r] = jnp.dot(weights.astype(BF16), values, preferred_element_type=F32)
            newtop[ch, pl.ds(r, 1)] = rows_to_lanes(top, eye)
            newsum[ch, pl.ds(r, 1)] = rows_to_lanes(total, eye)

    def o_copy(ch, k, dx):
        return pltpu.make_async_remote_copy(
            outb.at[ch, k, dx], xret[ch][k].at[dx - 1], o_send, o_recv.at[ch * NZ + k],
            device_id=node(mx + NX - dx, mz),
        )

    def s_copy(ch, k, dx):
        return pltpu.make_async_remote_copy(
            stato.at[ch, k, dx], xstat[ch][k].at[dx - 1], s_send, s_recv.at[ch * NZ + k],
            device_id=node(mx + NX - dx, mz),
        )

    token = lax.broadcasted_iota(I32, (CROWS, PAGE), 1)

    def attend(ch, k, dx):
        i = k * NX + dx
        blank = jnp.zeros((GROUP, HD), BF16)
        for slot in range(CAP):
            page = plan_s[i, 0, mx * 8 + L_PAGE + slot]
            usable = token < plan_s[i, 0, mx * 8 + L_TOK + slot]
            query = recvq[ch, k, dx, slot]
            scores = []
            for e in range(0, CHEADS, 2):
                low, high = query[e * GROUP : (e + 1) * GROUP], query[(e + 1) * GROUP : (e + 2) * GROUP]
                pair = jnp.concatenate(
                    [jnp.concatenate([low, blank], axis=1), jnp.concatenate([blank, high], axis=1)], axis=0
                )
                at = ch * CHEADS + e
                scores.append(
                    lax.dot_general(
                        pair,
                        kv_ref[page, :, at * HD : (at + 2) * HD],
                        (((1,), (1,)), ((), ())),
                        preferred_element_type=F32,
                    )
                )
            scores = jnp.where(usable, jnp.concatenate(scores, axis=0) * SCALE, NEG)
            top = jnp.max(scores, axis=1, keepdims=True)
            weights = jnp.where(usable, jnp.exp(scores - top), 0.0)
            total = jnp.sum(weights, axis=1, keepdims=True)
            rounded = weights.astype(BF16)
            for e in range(0, CHEADS, 2):
                at = KVH + ch * CHEADS + e
                mixed = jnp.dot(
                    rounded[e * GROUP : (e + 2) * GROUP],
                    kv_ref[page, :, at * HD : (at + 2) * HD],
                    preferred_element_type=F32,
                ).astype(BF16)
                outb[ch, k, dx, slot, e * GROUP : (e + 1) * GROUP] = mixed[:GROUP, :HD]
                outb[ch, k, dx, slot, (e + 1) * GROUP : (e + 2) * GROUP] = mixed[GROUP:, HD:]
            stato[ch, k, dx, slot : slot + 1] = rows_to_lanes(top, eye)
            stato[ch, k, dx, CAP + slot : CAP + slot + 1] = rows_to_lanes(total, eye)

    def work(ch, k):
        @pl.loop(0, NX)
        def _(dx):
            @pl.when(dx == 1)
            def _():
                drain(recvq.at[ch, k, pl.ds(1, NX - 1)], x_recv.at[ch * NZ + k])

            attend(ch, k, dx)

    def give(ch, k):
        @pl.loop(1, NX)
        def _(dx):
            o_copy(ch, k, dx).start()
            s_copy(ch, k, dx).start()

    def x_parts(ch, k, r):
        parts = []
        for dx in range(NX):
            ids = [plan_s[k * NX, 0, (mx + dx) % NX * 8 + L_ID + slot] for slot in range(CAP)]
            second = ids[1] == r
            slot = jnp.where(second, 1, 0)
            here = (ids[0] == r) | second
            if dx == 0:
                values, stat = outb[ch, k, 0, slot], stato[ch, k, 0]
            else:
                values, stat = xret[ch][k][dx - 1, slot], xstat[ch][k][dx - 1]
            top = jnp.where(second, stat[1:2], stat[0:1])
            count = jnp.where(second, stat[3:4], stat[2:3])
            parts.append((values, jnp.where(here, top, NEG), jnp.where(here, count, 0.0), here))
        return parts

    def merge(parts, new):
        peak = parts[0][1]
        for part in parts[1:]:
            peak = jnp.maximum(peak, part[1])
        if new is not None:
            peak = jnp.maximum(peak, new[1])
        shares = []
        total = jnp.zeros((1, 128), F32)
        for _, top, count, here in parts:
            share = jnp.exp(top - peak)
            if here is not None:
                share = jnp.where(here, share, 0.0)
            shares.append(share)
            total = total + share * count
        sources = [part[0] for part in parts]
        if new is not None:
            share = jnp.exp(new[1] - peak)
            total = total + share * new[2]
            shares = [one / total for one in shares + [share]]
            sources.append(new[0])
        result = None
        for share, source in zip(shares, sources):
            term = lanes_to_rows(share, eye) * source.astype(F32)
            result = term if result is None else result + term
        return result, peak, total

    def brought(ch, slot, half, rr):
        stat = cstat[ch][slot]
        return (
            chain[ch][slot][half * HALF + rr],
            stat[half, pl.ds(rr, 1), :],
            stat[half, pl.ds(HALF + rr, 1), :],
            None,
        )

    def x_done(ch, k):
        drain(xret[ch][k], o_recv.at[ch * NZ + k])
        drain(xstat[ch][k], s_recv.at[ch * NZ + k])

    def c_copies(ch, k, half):
        part = pl.ds(half * HALF, HALF)
        inward = k - 1 if k < 4 or (k == 4 and half == 0) else k + 1
        to = node(mx, mz + NZ - 1) if inward < k else node(mx, mz + 1)
        got = ch * (NZ + 1) + inward
        return [
            pltpu.make_async_remote_copy(
                dense[ch][k].at[part], chain[ch][inward].at[part], c_send, c_recv.at[got, half],
                device_id=to,
            ),
            pltpu.make_async_remote_copy(
                dstat[ch][k].at[half], cstat[ch][inward].at[half], cs_send, cs_recv.at[got, half],
                device_id=to,
            ),
        ]

    def link(ch, *order):
        for k in dict.fromkeys(k for k, _ in order):
            x_done(ch, k)
        for k, half in order:
            if k == 3 and half == 0 or k == 5 and half == 1:
                outer = 4
            elif k in (1, 2):
                outer = k + 1
            elif k in (6, 7):
                outer = k - 1
            else:
                outer = None
            if outer is not None:
                for copy in c_copies(ch, outer, half):
                    copy.wait_recv()

            @pl.loop(0, HALF)
            def _(rr):
                parts = x_parts(ch, k, half * HALF + rr)
                if outer is not None:
                    parts.append(brought(ch, k, half, rr))
                result, peak, total = merge(parts, None)
                dense[ch][k][half * HALF + rr] = result.astype(BF16)
                dstat[ch][k][half, pl.ds(rr, 1), :] = peak
                dstat[ch][k][half, pl.ds(HALF + rr, 1), :] = total

            for copy in c_copies(ch, k, half):
                copy.start()

    def f_copy(ch, to):
        part = pl.ds(ch * CWIDTH, CWIDTH)
        return pltpu.make_async_remote_copy(
            fin.at[ch, to], out_ref.at[g, :, part], f_send, f_recv, device_id={"grp": to}
        )

    own_f = [
        pltpu.make_async_copy(fin.at[ch, g], out_ref.at[g, :, pl.ds(ch * CWIDTH, CWIDTH)], loc_sem.at[NCH + 3 + ch])
        for ch in range(NCH)
    ]

    def finish(ch):
        x_done(ch, 0)
        for half in range(2):
            for outer in (1, 7):
                for copy in c_copies(ch, outer, half):
                    copy.wait_recv()

            @pl.loop(0, HALF)
            def _(t):
                rr = (g + 1 + t) % HALF
                r = half * HALF + rr
                parts = x_parts(ch, 0, r) + [brought(ch, 0, half, rr), brought(ch, NZ, half, rr)]
                new = (newmix[ch, r], newtop[ch, pl.ds(r, 1), :], newsum[ch, pl.ds(r, 1), :])
                result, _, _ = merge(parts, new)
                pieces = [result[h * STEPS : (h + 1) * STEPS] for h in range(CHEADS * GQ)]
                fin[ch, r] = jnp.concatenate(pieces, axis=1).astype(BF16)

                @pl.when(r != g)
                def _():
                    f_copy(ch, r).start()

                @pl.when(r == g)
                def _():
                    own_f[ch].start()

    steps = [(0,), (1, 7), (2, 6), (3, 5), (4,)]

    def forward(ch, step, todo):
        pass_on(ch, step)
        if step == 3 and ch + 1 < NCH:
            begin(ch + 1)
        for k in steps[step]:
            spread(ch, k)
        for one, k in todo:
            work(one, k)

    arrive(0)
    begin(0)
    own_plan.wait()
    spread(0, 0)
    arrive(1)
    spread(1, 0)
    pass_on(0, 1)

    drain(plan_in.at[pl.ds(0, NC - 1)], pl_recv)
    own_p.wait()
    plan_read = pltpu.make_async_copy(plan_in, plan_s, loc_sem.at[NCH + 2])
    plan_read.start()
    plan_read.wait()
    spread(0, 1)
    spread(0, 7)
    kv_copy.wait()
    work(0, 0)
    give(0, 0)
    forward(0, 2, [(1, 0)])
    own_n.wait()

    drain(newv.at[pl.ds(0, NG - 1)], gn_recv)
    forward(0, 3, [(0, 1), (0, 7)])
    forward(0, 4, [(0, 2), (0, 6)])
    forward(1, 1, [(0, 3), (0, 5)])
    give(0, 3)
    forward(1, 2, [(0, 4)])
    give(0, 4)
    give(0, 5)
    forward(1, 3, [(1, 1), (1, 7)])
    link(0, (4, 0), (4, 1))
    forward(1, 4, [(1, 2), (1, 6)])
    give(0, 2)
    give(0, 6)
    link(0, (3, 1), (5, 0), (3, 0), (5, 1))
    work(1, 3)
    work(1, 5)
    give(0, 1)
    give(0, 7)
    work(1, 4)
    give(1, 4)
    link(0, (2, 1), (6, 0), (2, 0), (6, 1))
    give(1, 3)
    give(1, 5)
    link(1, (4, 0), (4, 1))
    link(0, (1, 1), (7, 0), (1, 0), (7, 1))
    give(1, 2)
    give(1, 6)
    link(1, (3, 1), (5, 0), (3, 0), (5, 1))
    give(1, 1)
    give(1, 7)
    new_tokens(0)
    finish(0)
    link(1, (2, 1), (6, 0), (2, 0), (6, 1))
    give(1, 0)
    new_tokens(1)
    link(1, (1, 1), (7, 0), (1, 0), (7, 1))
    finish(1)

    for ch in range(NCH):
        own_f[ch].wait()
    drain(out_ref.at[pl.ds(0, NG - 1)], f_recv)
    drain(qs.at[pl.ds(0, NG - 1)], gq_send)
    drain(newv.at[pl.ds(0, NG - 1)], gn_send)
    drain(plan_in.at[pl.ds(0, NC - 1)], pl_send)
    drain(recvq.at[:, pl.ds(0, NZ - 1)], ag_send)
    drain(xsend, x_send)
    drain(xsend, o_send)
    drain(stato.at[:, :, pl.ds(1, NX - 1)], s_send)
    drain(recvq.at[:, pl.ds(0, NZ - 1)], c_send)
    drain(newmix.at[0, pl.ds(0, NZ - 1), pl.ds(0, 16 * NCH)], cs_send)
    drain(fin.at[:, pl.ds(0, NG - 1)], f_send)


def per_device(queries, new_kv, kv_cache, page_owner, page_index, lengths):
    dma = pltpu.SemaphoreType.DMA
    vmem = pl.BlockSpec(memory_space=pltpu.VMEM)
    smem = pl.BlockSpec(memory_space=pltpu.SMEM)
    hbm = pl.BlockSpec(memory_space=pl.ANY)
    block = pltpu.VMEM((REQ, CROWS, HD), BF16)
    return pl.pallas_call(
        kernel,
        out_shape=jax.ShapeDtypeStruct((REQ, STEPS, KVH * GQ * HD), BF16),
        in_specs=[vmem, vmem, smem, smem, smem, hbm],
        out_specs=hbm,
        scratch_shapes=[
            pltpu.VMEM((PAGES, PAGE, 2 * KVH * HD), BF16),
            *[block] * (NCH * NZ),
            *[pltpu.VMEM((NX - 1, CAP, CROWS, HD), BF16)] * (NCH * NZ),
            *[pltpu.VMEM((NX - 1, 2 * CAP, 128), F32)] * (NCH * NZ),
            *[block] * (NCH * NZ),
            *[pltpu.VMEM((2, 8, 128), F32)] * (NCH * NZ),
            *[block] * (NCH * (NZ + 1)),
            *[pltpu.VMEM((2, 8, 128), F32)] * (NCH * (NZ + 1)),
            pltpu.VMEM((REQ, ROWS, HD), BF16),
            pltpu.VMEM((REQ, STEPS, 2 * KVH * HD), BF16),
            pltpu.VMEM((NCH, NZ, NX - 1, CAP, CROWS, HD), BF16),
            pltpu.VMEM((NCH, NZ, NX, CAP, CROWS, HD), BF16),
            pltpu.VMEM((NCH, NZ, NX, CAP, CROWS, HD), BF16),
            pltpu.VMEM((NCH, NZ, NX, 2 * CAP, 128), F32),
            pltpu.VMEM((NZ, 1, 128), I32),
            pltpu.VMEM((NC, 1, 128), I32),
            pltpu.SMEM((NC, 1, 128), I32),
            pltpu.SMEM((1, 128), I32),
            pltpu.VMEM((NCH, REQ, CROWS, HD), F32),
            pltpu.VMEM((NCH, REQ, 128), F32),
            pltpu.VMEM((NCH, REQ, 128), F32),
            pltpu.VMEM((NCH, REQ, STEPS, CWIDTH), BF16),
            dma,
            dma((2 * NCH + 4,)),
            dma,
            dma((NCH,)),
            *[dma] * 4,
            dma,
            dma((NCH * NZ, 2)),
            *[dma, dma((NCH * NZ,))] * 3,
            *[dma, dma((NCH * (NZ + 1), 2))] * 2,
            *[dma] * 2,
        ],
        compiler_params=pltpu.CompilerParams(
            collective_id=0, has_side_effects=True, vmem_limit_bytes=56 * 1024 * 1024
        ),
        name="paged_decode",
    )(queries, new_kv, page_owner.T, page_index.reshape(REQ, SEL).T, lengths, kv_cache)


def solution(mesh):
    in_specs = (
        P(("grp", "cache"), None, None),
        P(("grp", "cache"), None, None),
        P(("grp", "cache"), None, None),
        P(("grp", "cache"), None),
        P(("grp", "cache"), None, None),
        P(("grp", "cache")),
    )
    out_specs = P(("grp", "cache"), None, None)
    return jax.shard_map(
        per_device, mesh=mesh, in_specs=in_specs, out_specs=out_specs, check_vma=False
    )
```

```python
import math

import jax
import jax.numpy as jnp
from jax import lax
from jax.experimental import pallas as pl
from jax.experimental.pallas import tpu as pltpu
from jax.sharding import PartitionSpec as P

KVH = 8
HD = 128
GQ = 8
STEPS = 4
PAGE = 128
SEL = 4
NX = 4
NZ = 8
NG = 8
NC = NX * NZ
REQ = 8
CAP = 2
PAGES = 16
GROUP = STEPS * GQ
ROWS = KVH * GROUP
HALF = REQ // 2
NCH = 2
CROWS = ROWS // NCH
CHEADS = KVH // NCH
CWIDTH = CHEADS * GQ * HD
NEG = -1e30
SCALE = 1.0 / math.sqrt(HD)
BF16 = jnp.bfloat16
F32 = jnp.float32
I32 = jnp.int32

L_REQ, L_PAGE, L_TOK, L_ID = 0, 2, 4, 6


def rows_to_lanes(column, eye):
    return jnp.sum(jnp.where(eye, jnp.broadcast_to(column, (CROWS, 128)), 0.0), axis=0, keepdims=True)


def lanes_to_rows(line, eye):
    return jnp.sum(jnp.where(eye, jnp.broadcast_to(line, (CROWS, 128)), 0.0), axis=1, keepdims=True)


def kernel(q_hbm, new_ref, owner_ref, page_ref, length_ref, kv_hbm, out_ref, kv_ref, *rest):
    rest = list(rest)

    def take(count):
        front = rest[:count]
        del rest[:count]
        return front

    def take_each(count):
        return [take(count) for _ in range(NCH)]

    ag, xret, xstat, dense, dstat = (take_each(NZ) for _ in range(5))
    chain, cstat = (take_each(NZ + 1) for _ in range(2))
    q_ref, qs, newv, xsend, recvq, outb, stato, plan_out, plan_in, plan_s, own_s, newmix, newtop, newsum, fin = take(15)
    kv_sem, loc_sem, gq_send, gq_recv, gn_send, gn_recv, pl_send, pl_recv = take(8)
    ag_send, ag_recv, x_send, x_recv, o_send, o_recv, s_send, s_recv = take(8)
    c_send, c_recv, cs_send, cs_recv, f_send, f_recv = take(6)

    g = lax.axis_index("grp")
    c = lax.axis_index("cache")
    mx, mz = c // NZ, c % NZ

    def node(x, z):
        return {"cache": (x % NX) * NZ + z % NZ}

    q_copy = pltpu.make_async_copy(q_hbm, q_ref, loc_sem.at[2 * NCH + 4])
    q_copy.start()

    barrier = pltpu.get_barrier_semaphore()

    @pl.loop(1, NG)
    def _(i):
        pl.semaphore_signal(barrier, inc=1, device_id={"grp": (g + i) % NG})

    @pl.loop(1, NC)
    def _(i):
        pl.semaphore_signal(barrier, inc=1, device_id={"cache": (c + i) % NC})

    kv_copy = pltpu.make_async_copy(kv_hbm, kv_ref, kv_sem)
    kv_copy.start()

    def make_rows(ch):
        @pl.loop(0, REQ)
        def _(r):
            wide = q_ref[r, :, ch * CWIDTH : (ch + 1) * CWIDTH].astype(F32)
            rows = [wide[:, h * HD : (h + 1) * HD] for h in range(CHEADS * GQ)]
            qs[r, ch * CROWS : (ch + 1) * CROWS] = jnp.concatenate(rows, axis=0).astype(BF16)

    q_copy.wait()
    make_rows(0)
    pl.semaphore_wait(barrier, NG - 1 + NC - 1)

    def drain(ref, sem):
        pltpu.make_async_copy(ref, ref, sem).wait()

    def gq_copy(ch, i):
        part = pl.ds(ch * CROWS, CROWS)
        src, dst = (g + i) % NG, g
        return pltpu.make_async_remote_copy(
            qs.at[src, part], ag[ch][0].at[dst], gq_send, gq_recv.at[ch],
            device_id={"grp": (g + i) % NG},
        )

    def gn_copy(i):
        src, dst = (g + i) % NG, g
        return pltpu.make_async_remote_copy(
            new_ref.at[src], newv.at[dst], gn_send, gn_recv, device_id={"grp": (g + i) % NG}
        )

    def plan_copy(i):
        k, dx = i // NX, i % NX
        return pltpu.make_async_remote_copy(
            plan_out.at[(mz + k) % NZ], plan_in.at[i], pl_send, pl_recv, device_id=node(mx + dx, mz + k)
        )

    own_q = [
        pltpu.make_async_copy(qs.at[g, pl.ds(ch * CROWS, CROWS)], ag[ch][0].at[g], loc_sem.at[ch])
        for ch in range(NCH)
    ]
    own_n = pltpu.make_async_copy(new_ref.at[g], newv.at[g], loc_sem.at[NCH])
    own_p = pltpu.make_async_copy(plan_out.at[mz], plan_in.at[0], loc_sem.at[NCH + 1])
    for ch in range(NCH):
        if ch > 0:
            make_rows(ch)
        own_q[ch].start()

        @pl.loop(1, NG)
        def _(i):
            gq_copy(ch, i).start()

        if ch == 0:
            entry = lax.broadcasted_iota(I32, (1, 128), 1)
            owner_row = jnp.full((1, 128), -1, I32)
            page_row = jnp.zeros((1, 128), I32)
            tok_row = jnp.zeros((1, 128), I32)
            for r in range(REQ):
                for s in range(SEL):
                    at = entry == r * SEL + s
                    owner_row = jnp.where(at, owner_ref[s, r], owner_row)
                    page_row = jnp.where(at, page_ref[s, r], page_row)
                    tok_row = jnp.where(at, jnp.clip(length_ref[r] - s * PAGE, 0, PAGE), tok_row)

            shape = (NZ, 128)
            lane = lax.broadcasted_iota(I32, shape, 1)
            row = lax.broadcasted_iota(I32, shape, 0)
            owners = jnp.broadcast_to(owner_row, shape)
            pages = jnp.broadcast_to(page_row, shape)
            tokens = jnp.broadcast_to(tok_row, shape)
            plan = jnp.zeros(shape, I32)
            for x in range(NX):
                match = (owners == row + x * NZ) & (lane < NC)
                first = jnp.min(jnp.where(match, lane, 999), axis=1, keepdims=True)
                last = jnp.max(jnp.where(match, lane, -1), axis=1, keepdims=True)
                is0 = lane == first
                is1 = match & (lane == last) & (last > first)
                for slot, here in enumerate((is0, is1)):
                    for base, value in ((L_REQ, lane // SEL), (L_PAGE, pages), (L_TOK, tokens)):
                        picked = jnp.sum(jnp.where(here, value, 0), axis=1, keepdims=True)
                        plan = jnp.where(lane == x * 8 + base + slot, picked, plan)
                    found = jnp.max(jnp.where(here, lane // SEL, -1), axis=1, keepdims=True)
                    plan = jnp.where(lane == x * 8 + L_ID + slot, found, plan)
            for z in range(NZ):
                plan_out[z] = plan[z : z + 1]
            own_plan = pltpu.make_async_copy(plan_out.at[mz], own_s, loc_sem.at[2 * NCH + 3])
            own_plan.start()
            own_p.start()

            @pl.loop(1, NC)
            def _(i):
                plan_copy(i).start()

    own_n.start()

    @pl.loop(1, NG)
    def _(i):
        gn_copy(i).start()

    def right(ch, k, half):
        part = pl.ds(half * HALF, HALF)
        return pltpu.make_async_remote_copy(
            ag[ch][k].at[part], ag[ch][k + 1].at[part], ag_send,
            ag_recv.at[ch * NZ + k + 1, half], device_id=node(mx, mz + 1),
        )

    def left(ch, k, half):
        part = pl.ds(half * HALF, HALF)
        to = (k - 1) % NZ
        return pltpu.make_async_remote_copy(
            ag[ch][k].at[part], ag[ch][to].at[part], ag_send,
            ag_recv.at[ch * NZ + to, half], device_id=node(mx, mz + NZ - 1),
        )

    def arrive(ch):
        drain(ag[ch][0].at[pl.ds(0, NG - 1)], gq_recv.at[ch])
        own_q[ch].wait()

    def begin(ch):
        right(ch, 0, 0).start()
        left(ch, 0, 1).start()
        right(ch, 0, 1).start()
        left(ch, 0, 0).start()

    def pass_on(ch, step):
        for half_a, half_b in ((0, 1), (1, 0)):
            if step < 4:
                right(ch, step - 1, half_a).wait_recv()
                if step + 1 < 4 or half_a == 0:
                    right(ch, step, half_a).start()
                left(ch, (NZ - step + 1) % NZ, half_b).wait_recv()
                if step + 1 < 4 or half_b == 1:
                    left(ch, NZ - step, half_b).start()
        if step == 4:
            right(ch, 3, 0).wait_recv()
            left(ch, 5, 1).wait_recv()

    def x_copy(ch, k, dx):
        return pltpu.make_async_remote_copy(
            xsend.at[ch, k, dx - 1], recvq.at[ch, k, dx], x_send, x_recv.at[ch * NZ + k],
            device_id=node(mx + dx, mz),
        )

    def spread(ch, k):
        def wanted(to, slot):
            at = to * 8 + L_REQ + slot
            return own_s[0, at] if k == 0 else plan_s[k * NX, 0, at]

        @pl.loop(1, NX)
        def _(dx):
            to = (mx + dx) % NX
            for slot in range(CAP):
                xsend[ch, k, dx - 1, slot] = ag[ch][k][wanted(to, slot)]
            x_copy(ch, k, dx).start()

        for slot in range(CAP):
            recvq[ch, k, 0, slot] = ag[ch][k][wanted(mx, slot)]

    eye = lax.broadcasted_iota(I32, (CROWS, 128), 0) == lax.broadcasted_iota(I32, (CROWS, 128), 1)

    def new_tokens(ch):
        n_row = lax.broadcasted_iota(I32, (CROWS, STEPS * CHEADS), 0)
        n_col = lax.broadcasted_iota(I32, (CROWS, STEPS * CHEADS), 1)
        n_ok = (n_row // GROUP == n_col // STEPS) & (n_col % STEPS <= n_row % STEPS)

        @pl.loop(0, REQ)
        def _(r):
            wide = newv[r].astype(F32)
            pieces = [wide[:, e * HD : (e + 1) * HD] for e in range(2 * KVH)]
            keys = jnp.concatenate(pieces[ch * CHEADS : (ch + 1) * CHEADS], axis=0).astype(BF16)
            values = jnp.concatenate(pieces[KVH + ch * CHEADS : KVH + (ch + 1) * CHEADS], axis=0).astype(BF16)
            scores = lax.dot_general(
                ag[ch][0][r], keys, (((1,), (1,)), ((), ())), preferred_element_type=F32
            ) * SCALE
            scores = jnp.where(n_ok, scores, NEG)
            top = jnp.max(scores, axis=1, keepdims=True)
            weights = jnp.where(n_ok, jnp.exp(scores - top), 0.0)
            total = jnp.sum(weights, axis=1, keepdims=True)
            newmix[ch, r] = jnp.dot(weights.astype(BF16), values, preferred_element_type=F32)
            newtop[ch, pl.ds(r, 1)] = rows_to_lanes(top, eye)
            newsum[ch, pl.ds(r, 1)] = rows_to_lanes(total, eye)

    def o_copy(ch, k, dx):
        return pltpu.make_async_remote_copy(
            outb.at[ch, k, dx], xret[ch][k].at[dx - 1], o_send, o_recv.at[ch * NZ + k],
            device_id=node(mx + NX - dx, mz),
        )

    def s_copy(ch, k, dx):
        return pltpu.make_async_remote_copy(
            stato.at[ch, k, dx], xstat[ch][k].at[dx - 1], s_send, s_recv.at[ch * NZ + k],
            device_id=node(mx + NX - dx, mz),
        )

    token = lax.broadcasted_iota(I32, (CROWS, PAGE), 1)

    def attend(ch, k, dx):
        i = k * NX + dx
        blank = jnp.zeros((GROUP, HD), BF16)
        for slot in range(CAP):
            page = plan_s[i, 0, mx * 8 + L_PAGE + slot]
            usable = token < plan_s[i, 0, mx * 8 + L_TOK + slot]
            query = recvq[ch, k, dx, slot]
            scores = []
            for e in range(0, CHEADS, 2):
                low, high = query[e * GROUP : (e + 1) * GROUP], query[(e + 1) * GROUP : (e + 2) * GROUP]
                pair = jnp.concatenate(
                    [jnp.concatenate([low, blank], axis=1), jnp.concatenate([blank, high], axis=1)], axis=0
                )
                at = ch * CHEADS + e
                scores.append(
                    lax.dot_general(
                        pair,
                        kv_ref[page, :, at * HD : (at + 2) * HD],
                        (((1,), (1,)), ((), ())),
                        preferred_element_type=F32,
                    )
                )
            scores = jnp.where(usable, jnp.concatenate(scores, axis=0) * SCALE, NEG)
            top = jnp.max(scores, axis=1, keepdims=True)
            weights = jnp.where(usable, jnp.exp(scores - top), 0.0)
            total = jnp.sum(weights, axis=1, keepdims=True)
            rounded = weights.astype(BF16)
            for e in range(0, CHEADS, 2):
                at = KVH + ch * CHEADS + e
                mixed = jnp.dot(
                    rounded[e * GROUP : (e + 2) * GROUP],
                    kv_ref[page, :, at * HD : (at + 2) * HD],
                    preferred_element_type=F32,
                ).astype(BF16)
                outb[ch, k, dx, slot, e * GROUP : (e + 1) * GROUP] = mixed[:GROUP, :HD]
                outb[ch, k, dx, slot, (e + 1) * GROUP : (e + 2) * GROUP] = mixed[GROUP:, HD:]
            stato[ch, k, dx, slot : slot + 1] = rows_to_lanes(top, eye)
            stato[ch, k, dx, CAP + slot : CAP + slot + 1] = rows_to_lanes(total, eye)

    def work(ch, k):
        @pl.loop(0, NX)
        def _(dx):
            @pl.when(dx == 1)
            def _():
                drain(recvq.at[ch, k, pl.ds(1, NX - 1)], x_recv.at[ch * NZ + k])

            attend(ch, k, dx)

    def give(ch, k):
        @pl.loop(1, NX)
        def _(dx):
            o_copy(ch, k, dx).start()
            s_copy(ch, k, dx).start()

    def x_parts(ch, k, r):
        parts = []
        for dx in range(NX):
            ids = [plan_s[k * NX, 0, (mx + dx) % NX * 8 + L_ID + slot] for slot in range(CAP)]
            second = ids[1] == r
            slot = jnp.where(second, 1, 0)
            here = (ids[0] == r) | second
            if dx == 0:
                values, stat = outb[ch, k, 0, slot], stato[ch, k, 0]
            else:
                values, stat = xret[ch][k][dx - 1, slot], xstat[ch][k][dx - 1]
            top = jnp.where(second, stat[1:2], stat[0:1])
            count = jnp.where(second, stat[3:4], stat[2:3])
            parts.append((values, jnp.where(here, top, NEG), jnp.where(here, count, 0.0), here))
        return parts

    def merge(parts, new):
        peak = parts[0][1]
        for part in parts[1:]:
            peak = jnp.maximum(peak, part[1])
        if new is not None:
            peak = jnp.maximum(peak, new[1])
        shares = []
        total = jnp.zeros((1, 128), F32)
        for _, top, count, here in parts:
            share = jnp.exp(top - peak)
            if here is not None:
                share = jnp.where(here, share, 0.0)
            shares.append(share)
            total = total + share * count
        sources = [part[0] for part in parts]
        if new is not None:
            share = jnp.exp(new[1] - peak)
            total = total + share * new[2]
            shares = [one / total for one in shares + [share]]
            sources.append(new[0])
        result = None
        for share, source in zip(shares, sources):
            term = lanes_to_rows(share, eye) * source.astype(F32)
            result = term if result is None else result + term
        return result, peak, total

    def brought(ch, slot, half, rr):
        stat = cstat[ch][slot]
        return (
            chain[ch][slot][half * HALF + rr],
            stat[half, pl.ds(rr, 1), :],
            stat[half, pl.ds(HALF + rr, 1), :],
            None,
        )

    def x_done(ch, k):
        drain(xret[ch][k], o_recv.at[ch * NZ + k])
        drain(xstat[ch][k], s_recv.at[ch * NZ + k])

    def c_copies(ch, k, half):
        part = pl.ds(half * HALF, HALF)
        inward = k - 1 if k < 4 or (k == 4 and half == 0) else k + 1
        to = node(mx, mz + NZ - 1) if inward < k else node(mx, mz + 1)
        got = ch * (NZ + 1) + inward
        return [
            pltpu.make_async_remote_copy(
                dense[ch][k].at[part], chain[ch][inward].at[part], c_send, c_recv.at[got, half],
                device_id=to,
            ),
            pltpu.make_async_remote_copy(
                dstat[ch][k].at[half], cstat[ch][inward].at[half], cs_send, cs_recv.at[got, half],
                device_id=to,
            ),
        ]

    def link(ch, *order):
        for k in dict.fromkeys(k for k, _ in order):
            x_done(ch, k)
        for k, half in order:
            if k == 3 and half == 0 or k == 5 and half == 1:
                outer = 4
            elif k in (1, 2):
                outer = k + 1
            elif k in (6, 7):
                outer = k - 1
            else:
                outer = None
            if outer is not None:
                for copy in c_copies(ch, outer, half):
                    copy.wait_recv()

            @pl.loop(0, HALF, unroll=4)
            def _(rr):
                parts = x_parts(ch, k, half * HALF + rr)
                if outer is not None:
                    parts.append(brought(ch, k, half, rr))
                result, peak, total = merge(parts, None)
                dense[ch][k][half * HALF + rr] = result.astype(BF16)
                dstat[ch][k][half, pl.ds(rr, 1), :] = peak
                dstat[ch][k][half, pl.ds(HALF + rr, 1), :] = total

            for copy in c_copies(ch, k, half):
                copy.start()

    def f_copy(ch, to):
        part = pl.ds(ch * CWIDTH, CWIDTH)
        return pltpu.make_async_remote_copy(
            fin.at[ch, to], out_ref.at[g, :, part], f_send, f_recv, device_id={"grp": to}
        )

    own_f = [
        pltpu.make_async_copy(fin.at[ch, g], out_ref.at[g, :, pl.ds(ch * CWIDTH, CWIDTH)], loc_sem.at[NCH + 3 + ch])
        for ch in range(NCH)
    ]

    def finish(ch):
        x_done(ch, 0)
        for half in range(2):
            for outer in (1, 7):
                for copy in c_copies(ch, outer, half):
                    copy.wait_recv()

            @pl.loop(0, HALF, unroll=4)
            def _(t):
                rr = (g + 1 + t) % HALF
                r = half * HALF + rr
                parts = x_parts(ch, 0, r) + [brought(ch, 0, half, rr), brought(ch, NZ, half, rr)]
                new = (newmix[ch, r], newtop[ch, pl.ds(r, 1), :], newsum[ch, pl.ds(r, 1), :])
                result, _, _ = merge(parts, new)
                pieces = [result[h * STEPS : (h + 1) * STEPS] for h in range(CHEADS * GQ)]
                fin[ch, r] = jnp.concatenate(pieces, axis=1).astype(BF16)

                @pl.when(r != g)
                def _():
                    f_copy(ch, r).start()

                @pl.when(r == g)
                def _():
                    own_f[ch].start()

    steps = [(0,), (1, 7), (2, 6), (3, 5), (4,)]

    def forward(ch, step, todo):
        pass_on(ch, step)
        if step == 3 and ch + 1 < NCH:
            begin(ch + 1)
        for k in steps[step]:
            spread(ch, k)
        for one, k in todo:
            work(one, k)

    arrive(0)
    begin(0)
    own_plan.wait()
    spread(0, 0)
    arrive(1)
    spread(1, 0)
    pass_on(0, 1)

    drain(plan_in.at[pl.ds(0, NC - 1)], pl_recv)
    own_p.wait()
    plan_read = pltpu.make_async_copy(plan_in, plan_s, loc_sem.at[NCH + 2])
    plan_read.start()
    plan_read.wait()
    spread(0, 1)
    spread(0, 7)
    kv_copy.wait()
    work(0, 0)
    give(0, 0)
    forward(0, 2, [(1, 0)])
    own_n.wait()

    drain(newv.at[pl.ds(0, NG - 1)], gn_recv)
    forward(0, 3, [(0, 1), (0, 7)])
    forward(0, 4, [(0, 2), (0, 6)])
    forward(1, 1, [(0, 3), (0, 5)])
    give(0, 3)
    forward(1, 2, [(0, 4)])
    give(0, 4)
    give(0, 5)
    forward(1, 3, [(1, 1), (1, 7)])
    link(0, (4, 0), (4, 1))
    forward(1, 4, [(1, 2), (1, 6)])
    give(0, 2)
    link(0, (3, 1), (5, 0), (3, 0), (5, 1))
    give(0, 6)
    work(1, 3)
    work(1, 5)
    work(1, 4)
    give(1, 4)
    give(0, 1)
    give(0, 7)
    link(0, (2, 1), (6, 0), (2, 0), (6, 1))
    give(1, 3)
    give(1, 5)
    link(1, (4, 0), (4, 1))
    link(0, (1, 1), (7, 0), (1, 0), (7, 1))
    give(1, 2)
    give(1, 6)
    link(1, (3, 1), (5, 0), (3, 0), (5, 1))
    give(1, 1)
    give(1, 7)
    new_tokens(0)
    finish(0)
    link(1, (2, 1), (6, 0), (2, 0), (6, 1))
    give(1, 0)
    new_tokens(1)
    link(1, (1, 1), (7, 0), (1, 0), (7, 1))
    finish(1)

    for ch in range(NCH):
        own_f[ch].wait()
    drain(out_ref.at[pl.ds(0, NG - 1)], f_recv)
    drain(qs.at[pl.ds(0, NG - 1)], gq_send)
    drain(newv.at[pl.ds(0, NG - 1)], gn_send)
    drain(plan_in.at[pl.ds(0, NC - 1)], pl_send)
    drain(recvq.at[:, pl.ds(0, NZ - 1)], ag_send)
    drain(xsend, x_send)
    drain(xsend, o_send)
    drain(stato.at[:, :, pl.ds(1, NX - 1)], s_send)
    drain(recvq.at[:, pl.ds(0, NZ - 1)], c_send)
    drain(newmix.at[0, pl.ds(0, NZ - 1), pl.ds(0, 16 * NCH)], cs_send)
    drain(fin.at[:, pl.ds(0, NG - 1)], f_send)


def per_device(queries, new_kv, kv_cache, page_owner, page_index, lengths):
    dma = pltpu.SemaphoreType.DMA
    smem = pl.BlockSpec(memory_space=pltpu.SMEM)
    hbm = pl.BlockSpec(memory_space=pl.ANY)
    block = pltpu.VMEM((REQ, CROWS, HD), BF16)
    return pl.pallas_call(
        kernel,
        out_shape=jax.ShapeDtypeStruct((REQ, STEPS, KVH * GQ * HD), BF16),
        in_specs=[hbm, hbm, smem, smem, smem, hbm],
        out_specs=hbm,
        scratch_shapes=[
            pltpu.VMEM((PAGES, PAGE, 2 * KVH * HD), BF16),
            *[block] * (NCH * NZ),
            *[pltpu.VMEM((NX - 1, CAP, CROWS, HD), BF16)] * (NCH * NZ),
            *[pltpu.VMEM((NX - 1, 2 * CAP, 128), F32)] * (NCH * NZ),
            *[block] * (NCH * NZ),
            *[pltpu.VMEM((2, 8, 128), F32)] * (NCH * NZ),
            *[block] * (NCH * (NZ + 1)),
            *[pltpu.VMEM((2, 8, 128), F32)] * (NCH * (NZ + 1)),
            pltpu.VMEM((REQ, STEPS, KVH * GQ * HD), BF16),
            pltpu.VMEM((REQ, ROWS, HD), BF16),
            pltpu.VMEM((REQ, STEPS, 2 * KVH * HD), BF16),
            pltpu.VMEM((NCH, NZ, NX - 1, CAP, CROWS, HD), BF16),
            pltpu.VMEM((NCH, NZ, NX, CAP, CROWS, HD), BF16),
            pltpu.VMEM((NCH, NZ, NX, CAP, CROWS, HD), BF16),
            pltpu.VMEM((NCH, NZ, NX, 2 * CAP, 128), F32),
            pltpu.VMEM((NZ, 1, 128), I32),
            pltpu.VMEM((NC, 1, 128), I32),
            pltpu.SMEM((NC, 1, 128), I32),
            pltpu.SMEM((1, 128), I32),
            pltpu.VMEM((NCH, REQ, CROWS, HD), F32),
            pltpu.VMEM((NCH, REQ, 128), F32),
            pltpu.VMEM((NCH, REQ, 128), F32),
            pltpu.VMEM((NCH, REQ, STEPS, CWIDTH), BF16),
            dma,
            dma((2 * NCH + 5,)),
            dma,
            dma((NCH,)),
            *[dma] * 4,
            dma,
            dma((NCH * NZ, 2)),
            *[dma, dma((NCH * NZ,))] * 3,
            *[dma, dma((NCH * (NZ + 1), 2))] * 2,
            *[dma] * 2,
        ],
        compiler_params=pltpu.CompilerParams(
            collective_id=0, has_side_effects=True, vmem_limit_bytes=56 * 1024 * 1024
        ),
        name="paged_decode",
    )(queries, new_kv, page_owner.T, page_index.reshape(REQ, SEL).T, lengths, kv_cache)


def solution(mesh):
    in_specs = (
        P(("grp", "cache"), None, None),
        P(("grp", "cache"), None, None),
        P(("grp", "cache"), None, None),
        P(("grp", "cache"), None),
        P(("grp", "cache"), None, None),
        P(("grp", "cache")),
    )
    out_specs = P(("grp", "cache"), None, None)
    return jax.shard_map(
        per_device, mesh=mesh, in_specs=in_specs, out_specs=out_specs, check_vma=False
    )
```

```python
import math

import jax
import jax.numpy as jnp
from jax import lax
from jax.experimental import pallas as pl
from jax.experimental.pallas import tpu as pltpu
from jax.sharding import PartitionSpec as P

KVH = 8
HD = 128
GQ = 8
STEPS = 4
PAGE = 128
SEL = 4
NX = 4
NZ = 8
NG = 8
NC = NX * NZ
REQ = 8
CAP = 2
PAGES = 16
GROUP = STEPS * GQ
ROWS = KVH * GROUP
HALF = REQ // 2
NCH = 2
CROWS = ROWS // NCH
CHEADS = KVH // NCH
CWIDTH = CHEADS * GQ * HD
NEG = -1e30
SCALE = 1.0 / math.sqrt(HD)
BF16 = jnp.bfloat16
F32 = jnp.float32
I32 = jnp.int32

L_REQ, L_PAGE, L_TOK, L_ID = 0, 2, 4, 6


def rows_to_lanes(column, eye):
    return jnp.sum(jnp.where(eye, jnp.broadcast_to(column, (CROWS, 128)), 0.0), axis=0, keepdims=True)


def lanes_to_rows(line, eye):
    return jnp.sum(jnp.where(eye, jnp.broadcast_to(line, (CROWS, 128)), 0.0), axis=1, keepdims=True)


def kernel(q_hbm, new_ref, owner_ref, page_ref, length_ref, kv_hbm, out_ref, kv_ref, *rest):
    rest = list(rest)

    def take(count):
        front = rest[:count]
        del rest[:count]
        return front

    def take_each(count):
        return [take(count) for _ in range(NCH)]

    ag, xret, xstat, dense, dstat = (take_each(NZ) for _ in range(5))
    chain, cstat = (take_each(NZ + 1) for _ in range(2))
    q_ref, qs, newv, xsend, recvq, outb, stato, plan_out, plan_in, plan_s, own_s, newmix, newtop, newsum, fin = take(15)
    kv_sem, loc_sem, gq_send, gq_recv, gn_send, gn_recv, pl_send, pl_recv = take(8)
    ag_send, ag_recv, x_send, x_recv, o_send, o_recv, s_send, s_recv = take(8)
    c_send, c_recv, cs_send, cs_recv, f_send, f_recv = take(6)

    g = lax.axis_index("grp")
    c = lax.axis_index("cache")
    mx, mz = c // NZ, c % NZ

    def node(x, z):
        return {"cache": (x % NX) * NZ + z % NZ}

    q_copy = pltpu.make_async_copy(q_hbm, q_ref, loc_sem.at[2 * NCH + 4])
    q_copy.start()

    barrier = pltpu.get_barrier_semaphore()

    @pl.loop(1, NG)
    def _(i):
        pl.semaphore_signal(barrier, inc=1, device_id={"grp": (g + i) % NG})

    @pl.loop(1, NC)
    def _(i):
        pl.semaphore_signal(barrier, inc=1, device_id={"cache": (c + i) % NC})

    kv_copy = pltpu.make_async_copy(kv_hbm, kv_ref, kv_sem)
    kv_copy.start()

    def make_rows(ch):
        @pl.loop(0, REQ)
        def _(r):
            wide = q_ref[r, :, ch * CWIDTH : (ch + 1) * CWIDTH].astype(F32)
            rows = [wide[:, h * HD : (h + 1) * HD] for h in range(CHEADS * GQ)]
            qs[r, ch * CROWS : (ch + 1) * CROWS] = jnp.concatenate(rows, axis=0).astype(BF16)

    q_copy.wait()
    make_rows(0)
    pl.semaphore_wait(barrier, NG - 1 + NC - 1)

    def drain(ref, sem):
        pltpu.make_async_copy(ref, ref, sem).wait()

    def gq_copy(ch, i):
        part = pl.ds(ch * CROWS, CROWS)
        src, dst = (g + i) % NG, g
        return pltpu.make_async_remote_copy(
            qs.at[src, part], ag[ch][0].at[dst], gq_send, gq_recv.at[ch],
            device_id={"grp": (g + i) % NG},
        )

    def gn_copy(i):
        src, dst = (g + i) % NG, g
        return pltpu.make_async_remote_copy(
            new_ref.at[src], newv.at[dst], gn_send, gn_recv, device_id={"grp": (g + i) % NG}
        )

    def plan_copy(i):
        k, dx = i // NX, i % NX
        return pltpu.make_async_remote_copy(
            plan_out.at[(mz + k) % NZ], plan_in.at[i], pl_send, pl_recv, device_id=node(mx + dx, mz + k)
        )

    own_q = [
        pltpu.make_async_copy(qs.at[g, pl.ds(ch * CROWS, CROWS)], ag[ch][0].at[g], loc_sem.at[ch])
        for ch in range(NCH)
    ]
    own_n = pltpu.make_async_copy(new_ref.at[g], newv.at[g], loc_sem.at[NCH])
    own_p = pltpu.make_async_copy(plan_out.at[mz], plan_in.at[0], loc_sem.at[NCH + 1])
    for ch in range(NCH):
        if ch > 0:
            make_rows(ch)
        own_q[ch].start()

        @pl.loop(1, NG)
        def _(i):
            gq_copy(ch, i).start()

        if ch == 0:
            entry = lax.broadcasted_iota(I32, (1, 128), 1)
            owner_row = jnp.full((1, 128), -1, I32)
            page_row = jnp.zeros((1, 128), I32)
            tok_row = jnp.zeros((1, 128), I32)
            for r in range(REQ):
                for s in range(SEL):
                    at = entry == r * SEL + s
                    owner_row = jnp.where(at, owner_ref[s, r], owner_row)
                    page_row = jnp.where(at, page_ref[s, r], page_row)
                    tok_row = jnp.where(at, jnp.clip(length_ref[r] - s * PAGE, 0, PAGE), tok_row)

            shape = (NZ, 128)
            lane = lax.broadcasted_iota(I32, shape, 1)
            row = lax.broadcasted_iota(I32, shape, 0)
            owners = jnp.broadcast_to(owner_row, shape)
            pages = jnp.broadcast_to(page_row, shape)
            tokens = jnp.broadcast_to(tok_row, shape)
            plan = jnp.zeros(shape, I32)
            for x in range(NX):
                match = (owners == row + x * NZ) & (lane < NC)
                first = jnp.min(jnp.where(match, lane, 999), axis=1, keepdims=True)
                last = jnp.max(jnp.where(match, lane, -1), axis=1, keepdims=True)
                is0 = lane == first
                is1 = match & (lane == last) & (last > first)
                for slot, here in enumerate((is0, is1)):
                    for base, value in ((L_REQ, lane // SEL), (L_PAGE, pages), (L_TOK, tokens)):
                        picked = jnp.sum(jnp.where(here, value, 0), axis=1, keepdims=True)
                        plan = jnp.where(lane == x * 8 + base + slot, picked, plan)
                    found = jnp.max(jnp.where(here, lane // SEL, -1), axis=1, keepdims=True)
                    plan = jnp.where(lane == x * 8 + L_ID + slot, found, plan)
            for z in range(NZ):
                plan_out[z] = plan[z : z + 1]
            own_plan = pltpu.make_async_copy(plan_out.at[mz], own_s, loc_sem.at[2 * NCH + 3])
            own_plan.start()
            own_p.start()

            @pl.loop(1, NC)
            def _(i):
                plan_copy(i).start()

    own_n.start()

    @pl.loop(1, NG)
    def _(i):
        gn_copy(i).start()

    def right(ch, k, half):
        part = pl.ds(half * HALF, HALF)
        return pltpu.make_async_remote_copy(
            ag[ch][k].at[part], ag[ch][k + 1].at[part], ag_send,
            ag_recv.at[ch * NZ + k + 1, half], device_id=node(mx, mz + 1),
        )

    def left(ch, k, half):
        part = pl.ds(half * HALF, HALF)
        to = (k - 1) % NZ
        return pltpu.make_async_remote_copy(
            ag[ch][k].at[part], ag[ch][to].at[part], ag_send,
            ag_recv.at[ch * NZ + to, half], device_id=node(mx, mz + NZ - 1),
        )

    def arrive(ch):
        drain(ag[ch][0].at[pl.ds(0, NG - 1)], gq_recv.at[ch])
        own_q[ch].wait()

    def begin(ch):
        right(ch, 0, 0).start()
        left(ch, 0, 1).start()
        right(ch, 0, 1).start()
        left(ch, 0, 0).start()

    def pass_on(ch, step):
        for half_a, half_b in ((0, 1), (1, 0)):
            if step < 4:
                right(ch, step - 1, half_a).wait_recv()
                if step + 1 < 4 or half_a == 0:
                    right(ch, step, half_a).start()
                left(ch, (NZ - step + 1) % NZ, half_b).wait_recv()
                if step + 1 < 4 or half_b == 1:
                    left(ch, NZ - step, half_b).start()
        if step == 4:
            right(ch, 3, 0).wait_recv()
            left(ch, 5, 1).wait_recv()

    def x_copy(ch, k, dx):
        return pltpu.make_async_remote_copy(
            xsend.at[ch, k, dx - 1], recvq.at[ch, k, dx], x_send, x_recv.at[ch * NZ + k],
            device_id=node(mx + dx, mz),
        )

    def spread(ch, k):
        def wanted(to, slot):
            at = to * 8 + L_REQ + slot
            return own_s[0, at] if k == 0 else plan_s[k * NX, 0, at]

        @pl.loop(1, NX)
        def _(dx):
            to = (mx + dx) % NX
            for slot in range(CAP):
                xsend[ch, k, dx - 1, slot] = ag[ch][k][wanted(to, slot)]
            x_copy(ch, k, dx).start()

        for slot in range(CAP):
            recvq[ch, k, 0, slot] = ag[ch][k][wanted(mx, slot)]

    eye = lax.broadcasted_iota(I32, (CROWS, 128), 0) == lax.broadcasted_iota(I32, (CROWS, 128), 1)

    def new_tokens(ch):
        n_row = lax.broadcasted_iota(I32, (CROWS, STEPS * CHEADS), 0)
        n_col = lax.broadcasted_iota(I32, (CROWS, STEPS * CHEADS), 1)
        n_ok = (n_row // GROUP == n_col // STEPS) & (n_col % STEPS <= n_row % STEPS)

        @pl.loop(0, REQ)
        def _(r):
            wide = newv[r].astype(F32)
            pieces = [wide[:, e * HD : (e + 1) * HD] for e in range(2 * KVH)]
            keys = jnp.concatenate(pieces[ch * CHEADS : (ch + 1) * CHEADS], axis=0).astype(BF16)
            values = jnp.concatenate(pieces[KVH + ch * CHEADS : KVH + (ch + 1) * CHEADS], axis=0).astype(BF16)
            scores = lax.dot_general(
                ag[ch][0][r], keys, (((1,), (1,)), ((), ())), preferred_element_type=F32
            ) * SCALE
            scores = jnp.where(n_ok, scores, NEG)
            top = jnp.max(scores, axis=1, keepdims=True)
            weights = jnp.where(n_ok, jnp.exp(scores - top), 0.0)
            total = jnp.sum(weights, axis=1, keepdims=True)
            newmix[ch, r] = jnp.dot(weights.astype(BF16), values, preferred_element_type=F32)
            newtop[ch, pl.ds(r, 1)] = rows_to_lanes(top, eye)
            newsum[ch, pl.ds(r, 1)] = rows_to_lanes(total, eye)

    def o_copy(ch, k, dx):
        return pltpu.make_async_remote_copy(
            outb.at[ch, k, dx], xret[ch][k].at[dx - 1], o_send, o_recv.at[ch * NZ + k],
            device_id=node(mx + NX - dx, mz),
        )

    def s_copy(ch, k, dx):
        return pltpu.make_async_remote_copy(
            stato.at[ch, k, dx], xstat[ch][k].at[dx - 1], s_send, s_recv.at[ch * NZ + k],
            device_id=node(mx + NX - dx, mz),
        )

    token = lax.broadcasted_iota(I32, (CROWS, PAGE), 1)

    def attend(ch, k, dx):
        i = k * NX + dx
        blank = jnp.zeros((GROUP, HD), BF16)
        for slot in range(CAP):
            page = plan_s[i, 0, mx * 8 + L_PAGE + slot]
            usable = token < plan_s[i, 0, mx * 8 + L_TOK + slot]
            query = recvq[ch, k, dx, slot]
            scores = []
            for e in range(0, CHEADS, 2):
                low, high = query[e * GROUP : (e + 1) * GROUP], query[(e + 1) * GROUP : (e + 2) * GROUP]
                pair = jnp.concatenate(
                    [jnp.concatenate([low, blank], axis=1), jnp.concatenate([blank, high], axis=1)], axis=0
                )
                at = ch * CHEADS + e
                scores.append(
                    lax.dot_general(
                        pair,
                        kv_ref[page, :, at * HD : (at + 2) * HD],
                        (((1,), (1,)), ((), ())),
                        preferred_element_type=F32,
                    )
                )
            scores = jnp.where(usable, jnp.concatenate(scores, axis=0) * SCALE, NEG)
            top = jnp.max(scores, axis=1, keepdims=True)
            weights = jnp.where(usable, jnp.exp(scores - top), 0.0)
            total = jnp.sum(weights, axis=1, keepdims=True)
            rounded = weights.astype(BF16)
            for e in range(0, CHEADS, 2):
                at = KVH + ch * CHEADS + e
                mixed = jnp.dot(
                    rounded[e * GROUP : (e + 2) * GROUP],
                    kv_ref[page, :, at * HD : (at + 2) * HD],
                    preferred_element_type=F32,
                ).astype(BF16)
                outb[ch, k, dx, slot, e * GROUP : (e + 1) * GROUP] = mixed[:GROUP, :HD]
                outb[ch, k, dx, slot, (e + 1) * GROUP : (e + 2) * GROUP] = mixed[GROUP:, HD:]
            stato[ch, k, dx, slot : slot + 1] = rows_to_lanes(top, eye)
            stato[ch, k, dx, CAP + slot : CAP + slot + 1] = rows_to_lanes(total, eye)

    def work(ch, k):
        @pl.loop(0, NX)
        def _(dx):
            @pl.when(dx == 1)
            def _():
                drain(recvq.at[ch, k, pl.ds(1, NX - 1)], x_recv.at[ch * NZ + k])

            attend(ch, k, dx)

    def give(ch, k):
        @pl.loop(1, NX)
        def _(dx):
            o_copy(ch, k, dx).start()
            s_copy(ch, k, dx).start()

    def x_parts(ch, k, r):
        parts = []
        for dx in range(NX):
            ids = [plan_s[k * NX, 0, (mx + dx) % NX * 8 + L_ID + slot] for slot in range(CAP)]
            second = ids[1] == r
            slot = jnp.where(second, 1, 0)
            here = (ids[0] == r) | second
            if dx == 0:
                values, stat = outb[ch, k, 0, slot], stato[ch, k, 0]
            else:
                values, stat = xret[ch][k][dx - 1, slot], xstat[ch][k][dx - 1]
            top = jnp.where(second, stat[1:2], stat[0:1])
            count = jnp.where(second, stat[3:4], stat[2:3])
            parts.append((values, jnp.where(here, top, NEG), jnp.where(here, count, 0.0), here))
        return parts

    def merge(parts, new):
        peak = parts[0][1]
        for part in parts[1:]:
            peak = jnp.maximum(peak, part[1])
        if new is not None:
            peak = jnp.maximum(peak, new[1])
        shares = []
        total = jnp.zeros((1, 128), F32)
        for _, top, count, here in parts:
            share = jnp.exp(top - peak)
            if here is not None:
                share = jnp.where(here, share, 0.0)
            shares.append(share)
            total = total + share * count
        sources = [part[0] for part in parts]
        if new is not None:
            share = jnp.exp(new[1] - peak)
            total = total + share * new[2]
            shares = [one / total for one in shares + [share]]
            sources.append(new[0])
        result = None
        for share, source in zip(shares, sources):
            term = lanes_to_rows(share, eye) * source.astype(F32)
            result = term if result is None else result + term
        return result, peak, total

    def brought(ch, slot, half, rr):
        stat = cstat[ch][slot]
        return (
            chain[ch][slot][half * HALF + rr],
            stat[half, pl.ds(rr, 1), :],
            stat[half, pl.ds(HALF + rr, 1), :],
            None,
        )

    def x_done(ch, k):
        drain(xret[ch][k], o_recv.at[ch * NZ + k])
        drain(xstat[ch][k], s_recv.at[ch * NZ + k])

    def c_copies(ch, k, half):
        part = pl.ds(half * HALF, HALF)
        inward = k - 1 if k < 4 or (k == 4 and half == 0) else k + 1
        to = node(mx, mz + NZ - 1) if inward < k else node(mx, mz + 1)
        got = ch * (NZ + 1) + inward
        return [
            pltpu.make_async_remote_copy(
                dense[ch][k].at[part], chain[ch][inward].at[part], c_send, c_recv.at[got, half],
                device_id=to,
            ),
            pltpu.make_async_remote_copy(
                dstat[ch][k].at[half], cstat[ch][inward].at[half], cs_send, cs_recv.at[got, half],
                device_id=to,
            ),
        ]

    def link(ch, *order):
        for k in dict.fromkeys(k for k, _ in order):
            x_done(ch, k)
        for k, half in order:
            if k == 3 and half == 0 or k == 5 and half == 1:
                outer = 4
            elif k in (1, 2):
                outer = k + 1
            elif k in (6, 7):
                outer = k - 1
            else:
                outer = None
            if outer is not None:
                for copy in c_copies(ch, outer, half):
                    copy.wait_recv()

            @pl.loop(0, HALF, unroll=4)
            def _(rr):
                parts = x_parts(ch, k, half * HALF + rr)
                if outer is not None:
                    parts.append(brought(ch, k, half, rr))
                result, peak, total = merge(parts, None)
                dense[ch][k][half * HALF + rr] = result.astype(BF16)
                dstat[ch][k][half, pl.ds(rr, 1), :] = peak
                dstat[ch][k][half, pl.ds(HALF + rr, 1), :] = total

            for copy in c_copies(ch, k, half):
                copy.start()

    def f_copy(ch, to):
        part = pl.ds(ch * CWIDTH, CWIDTH)
        return pltpu.make_async_remote_copy(
            fin.at[ch, to], out_ref.at[g, :, part], f_send, f_recv, device_id={"grp": to}
        )

    own_f = [
        pltpu.make_async_copy(fin.at[ch, g], out_ref.at[g, :, pl.ds(ch * CWIDTH, CWIDTH)], loc_sem.at[NCH + 3 + ch])
        for ch in range(NCH)
    ]

    def finish(ch):
        x_done(ch, 0)
        for half in range(2):
            for outer in (1, 7):
                for copy in c_copies(ch, outer, half):
                    copy.wait_recv()

            @pl.loop(0, HALF, unroll=4)
            def _(t):
                rr = (g + 1 + t) % HALF
                r = half * HALF + rr
                parts = x_parts(ch, 0, r) + [brought(ch, 0, half, rr), brought(ch, NZ, half, rr)]
                new = (newmix[ch, r], newtop[ch, pl.ds(r, 1), :], newsum[ch, pl.ds(r, 1), :])
                result, _, _ = merge(parts, new)
                pieces = [result[h * STEPS : (h + 1) * STEPS] for h in range(CHEADS * GQ)]
                fin[ch, r] = jnp.concatenate(pieces, axis=1).astype(BF16)

                @pl.when(r != g)
                def _():
                    f_copy(ch, r).start()

                @pl.when(r == g)
                def _():
                    own_f[ch].start()

    steps = [(0,), (1, 7), (2, 6), (3, 5), (4,)]

    def forward(ch, step, todo):
        pass_on(ch, step)
        if step == 3 and ch + 1 < NCH:
            begin(ch + 1)
        for k in steps[step]:
            spread(ch, k)
        for one, k in todo:
            work(one, k)

    arrive(0)
    begin(0)
    own_plan.wait()
    spread(0, 0)
    arrive(1)
    spread(1, 0)
    pass_on(0, 1)

    drain(plan_in.at[pl.ds(0, NC - 1)], pl_recv)
    own_p.wait()
    plan_read = pltpu.make_async_copy(plan_in, plan_s, loc_sem.at[NCH + 2])
    plan_read.start()
    plan_read.wait()
    spread(0, 1)
    spread(0, 7)
    kv_copy.wait()
    work(0, 0)
    give(0, 0)
    forward(0, 2, [(1, 0)])
    own_n.wait()

    drain(newv.at[pl.ds(0, NG - 1)], gn_recv)
    forward(0, 3, [(0, 1), (0, 7)])
    forward(0, 4, [(0, 2), (0, 6)])
    forward(1, 1, [(0, 3), (0, 5)])
    give(0, 3)
    forward(1, 2, [(0, 4)])
    give(0, 4)
    give(0, 5)
    forward(1, 3, [(1, 1), (1, 7)])
    link(0, (4, 0), (4, 1))
    forward(1, 4, [(1, 2), (1, 6)])
    give(0, 2)
    link(0, (3, 1), (5, 0), (3, 0), (5, 1))
    give(0, 6)
    new_tokens(0)
    work(1, 3)
    work(1, 5)
    work(1, 4)
    give(1, 4)
    give(0, 1)
    give(0, 7)
    new_tokens(1)
    link(0, (2, 1), (6, 0), (2, 0), (6, 1))
    give(1, 3)
    give(1, 5)
    link(1, (4, 0), (4, 1))
    link(0, (1, 1), (7, 0), (1, 0), (7, 1))
    give(1, 2)
    give(1, 6)
    link(1, (3, 1), (5, 0), (3, 0), (5, 1))
    give(1, 1)
    give(1, 7)
    finish(0)
    link(1, (2, 1), (6, 0), (2, 0), (6, 1))
    give(1, 0)
    link(1, (1, 1), (7, 0), (1, 0), (7, 1))
    finish(1)

    for ch in range(NCH):
        own_f[ch].wait()
    drain(out_ref.at[pl.ds(0, NG - 1)], f_recv)
    drain(qs.at[pl.ds(0, NG - 1)], gq_send)
    drain(newv.at[pl.ds(0, NG - 1)], gn_send)
    drain(plan_in.at[pl.ds(0, NC - 1)], pl_send)
    drain(recvq.at[:, pl.ds(0, NZ - 1)], ag_send)
    drain(xsend, x_send)
    drain(xsend, o_send)
    drain(stato.at[:, :, pl.ds(1, NX - 1)], s_send)
    drain(recvq.at[:, pl.ds(0, NZ - 1)], c_send)
    drain(newmix.at[0, pl.ds(0, NZ - 1), pl.ds(0, 16 * NCH)], cs_send)
    drain(fin.at[:, pl.ds(0, NG - 1)], f_send)


def per_device(queries, new_kv, kv_cache, page_owner, page_index, lengths):
    dma = pltpu.SemaphoreType.DMA
    smem = pl.BlockSpec(memory_space=pltpu.SMEM)
    hbm = pl.BlockSpec(memory_space=pl.ANY)
    block = pltpu.VMEM((REQ, CROWS, HD), BF16)
    return pl.pallas_call(
        kernel,
        out_shape=jax.ShapeDtypeStruct((REQ, STEPS, KVH * GQ * HD), BF16),
        in_specs=[hbm, hbm, smem, smem, smem, hbm],
        out_specs=hbm,
        scratch_shapes=[
            pltpu.VMEM((PAGES, PAGE, 2 * KVH * HD), BF16),
            *[block] * (NCH * NZ),
            *[pltpu.VMEM((NX - 1, CAP, CROWS, HD), BF16)] * (NCH * NZ),
            *[pltpu.VMEM((NX - 1, 2 * CAP, 128), F32)] * (NCH * NZ),
            *[block] * (NCH * NZ),
            *[pltpu.VMEM((2, 8, 128), F32)] * (NCH * NZ),
            *[block] * (NCH * (NZ + 1)),
            *[pltpu.VMEM((2, 8, 128), F32)] * (NCH * (NZ + 1)),
            pltpu.VMEM((REQ, STEPS, KVH * GQ * HD), BF16),
            pltpu.VMEM((REQ, ROWS, HD), BF16),
            pltpu.VMEM((REQ, STEPS, 2 * KVH * HD), BF16),
            pltpu.VMEM((NCH, NZ, NX - 1, CAP, CROWS, HD), BF16),
            pltpu.VMEM((NCH, NZ, NX, CAP, CROWS, HD), BF16),
            pltpu.VMEM((NCH, NZ, NX, CAP, CROWS, HD), BF16),
            pltpu.VMEM((NCH, NZ, NX, 2 * CAP, 128), F32),
            pltpu.VMEM((NZ, 1, 128), I32),
            pltpu.VMEM((NC, 1, 128), I32),
            pltpu.SMEM((NC, 1, 128), I32),
            pltpu.SMEM((1, 128), I32),
            pltpu.VMEM((NCH, REQ, CROWS, HD), F32),
            pltpu.VMEM((NCH, REQ, 128), F32),
            pltpu.VMEM((NCH, REQ, 128), F32),
            pltpu.VMEM((NCH, REQ, STEPS, CWIDTH), BF16),
            dma,
            dma((2 * NCH + 5,)),
            dma,
            dma((NCH,)),
            *[dma] * 4,
            dma,
            dma((NCH * NZ, 2)),
            *[dma, dma((NCH * NZ,))] * 3,
            *[dma, dma((NCH * (NZ + 1), 2))] * 2,
            *[dma] * 2,
        ],
        compiler_params=pltpu.CompilerParams(
            collective_id=0, has_side_effects=True, vmem_limit_bytes=56 * 1024 * 1024
        ),
        name="paged_decode",
    )(queries, new_kv, page_owner.T, page_index.reshape(REQ, SEL).T, lengths, kv_cache)


def solution(mesh):
    in_specs = (
        P(("grp", "cache"), None, None),
        P(("grp", "cache"), None, None),
        P(("grp", "cache"), None, None),
        P(("grp", "cache"), None),
        P(("grp", "cache"), None, None),
        P(("grp", "cache")),
    )
    out_specs = P(("grp", "cache"), None, None)
    return jax.shard_map(
        per_device, mesh=mesh, in_specs=in_specs, out_specs=out_specs, check_vma=False
    )
```
